512 devices in a mesh: section: 8 (over y_hi, x), dp: 64 (over z, y_lo, core).
Axes of the slice: x: 4, y: 4 (y_hi: 2, y_lo: 2; y = y_hi * 2 + y_lo), z: 16, core: 2. Of those that a mesh axis runs over, the one named last changes fastest.
Arguments:
- acts: bfloat16 [8, 8704, 8192], P('section', 'dp'), may hold values from -6 to 6
- value_grad: bfloat16 [8, 8704, 512], P('section', 'dp'), may hold values from -6 to 6
- loss_weight: int32 [8, 8704], P('section', 'dp'), may hold values from 1 to 4
- value_weight: bfloat16 [8, 8192, 512], P('section', 'dp'), may hold values from -0.0625 to 0.0625
- down_master: float32 [8, 8192, 64], P('section', 'dp'), may hold values from -0.0625 to 0.0625
- down_first: float32 [8, 8192, 64], P('section', 'dp'), may hold values from -0.006 to 0.006
- down_second: float32 [8, 8192, 64], P('section', 'dp'), may hold values from 1e-06 to 0.0001
- up_master: float32 [8, 64, 512], P('section', 'dp'), may hold values from -0.75 to 0.75
- up_first: float32 [8, 64, 512], P('section', 'dp'), may hold values from -0.006 to 0.006
- up_second: float32 [8, 64, 512], P('section', 'dp'), may hold values from 1e-06 to 0.0001
- step_count: int32 [1], replicated, may hold values from 1 to 99
Outputs:
- upstream_grad: bfloat16 [8, 8704, 8192], P('section', 'dp')
- refreshed: bfloat16 [8, 8704, 512], P('section', 'dp')
- down_new: float32 [8, 8192, 64], P('section', 'dp')
- down_first_new: float32 [8, 8192, 64], P('section', 'dp')
- down_second_new: float32 [8, 8192, 64], P('section', 'dp')
- up_new: float32 [8, 64, 512], P('section', 'dp')
- up_first_new: float32 [8, 64, 512], P('section', 'dp')
- up_second_new: float32 [8, 64, 512], P('section', 'dp')
The draws below stay inside these ranges and needn't reach their ends.
All inputs are finite; a program needn't handle non-finite values.
Results may differ from the reference program's by a relative error of at most 0.007.
The reference program's roundings to bfloat16 on the way (of `scaled`, `down_cur`, `mid`, `low` and `input_grad`) count: a program that leaves them out, or rounds other values in their place, can miss the bound.
Values may be sent and summed in bfloat16 or wider, within the bound.
No kernel may reach another device: no remote copies, remote signals or barrier semaphores. Data moves between devices by JAX's collectives and lax.ppermute only.
A program may use at most 64 MiB of HBM per device.

```python
import math
import jax
import jax.numpy as jnp
from jax import lax

D = 8192
KVW = 512
RANK = 64
TOKENS = 8704
SECTIONS = 8


def touch_ends(values, rng, low, largest):
    shape = values.shape
    index_at = [jax.random.randint(jax.random.fold_in(rng, axis), (), 0, shape[axis]) for axis in range(len(shape))]
    values = values.at[tuple(index_at)].set(low)
    longest = shape.index(max(shape))
    index_at[longest] = (index_at[longest] + 1) % shape[longest]
    return values.at[tuple(index_at)].set(largest)


def level_of(rng, extent, shards, low, high):
    level, own = 1.0, jax.random.fold_in(rng, 6)
    for position, blocks in shards:
        heights = jnp.exp(jax.random.uniform(jax.random.fold_in(own, position), (blocks,), jnp.float32, low / len(shards), high / len(shards)))
        level = level * jnp.repeat(heights, extent[position] // blocks).reshape([-1 if axis == position else 1 for axis in range(len(extent))])
    return level


def noise(rng, extent, width, bound, pieces=(), held_as=jnp.bfloat16):
    drawn = jax.random.normal(rng, extent, jnp.float32) * width
    if len(pieces) > 0:
        drawn = level_of(rng, extent, pieces, -0.22, 0.18) * drawn
    return jnp.clip(drawn, min=-bound, max=bound).astype(held_as)


def setup_inputs(seed: int = 0) -> dict:
    keys = jax.random.split(jax.random.key(seed), 12)
    return {
        "acts": noise(keys[0], (SECTIONS, TOKENS, D), 1.0, 6.0, ((0, 8), (1, 64))),
        "value_grad": noise(keys[1], (SECTIONS, TOKENS, KVW), 1.0, 6.0, ((0, 8), (1, 64))),
        "loss_weight": touch_ends(jax.random.randint(keys[2], (SECTIONS, TOKENS), 1, 5), jax.random.fold_in(keys[2], 1), 1, 4).astype(jnp.int32),
        "value_weight": noise(keys[3], (SECTIONS, D, KVW), D ** -0.5, 0.0625, ((0, 8), (1, 64))),
        "down_master": noise(keys[4], (SECTIONS, D, RANK), D ** -0.5, 0.0625, ((0, 8), (1, 64)), jnp.float32),
        "down_first": noise(keys[5], (SECTIONS, D, RANK), 0.001, 0.006, ((0, 8), (1, 64)), jnp.float32),
        "down_second": jnp.clip(jnp.exp(math.log(0.0001) - 4.6051702 * jax.random.uniform(keys[6], (SECTIONS, D, RANK), jnp.float32) ** level_of(keys[6], (SECTIONS, D, RANK), ((0, 8), (1, 64)), -0.2, 0.2)), 9.999999974752427e-07, 0.0001),
        "up_master": noise(keys[7], (SECTIONS, RANK, KVW), RANK ** -0.5, 0.75, ((0, 8), (1, 64)), jnp.float32),
        "up_first": noise(keys[8], (SECTIONS, RANK, KVW), 0.001, 0.006, ((0, 8), (1, 64)), jnp.float32),
        "up_second": jnp.clip(jnp.exp(math.log(0.0001) - 4.6051702 * jax.random.uniform(keys[9], (SECTIONS, RANK, KVW), jnp.float32) ** level_of(keys[9], (SECTIONS, RANK, KVW), ((0, 8), (1, 64)), -0.2, 0.2)), 9.999999974752427e-07, 0.0001),
        "step_count": jax.random.randint(keys[10], (1,), 1, 100).astype(jnp.int32),
    }


adapter_scale = 2.0
beta_one = 0.9
beta_two = 0.999
learn_rate = 0.05
adam_eps = 1e-08

def adam_update(master, first, second, grad, count):
    first_new = beta_one * first + (1.0 - beta_one) * grad
    second_new = beta_two * second + (1.0 - beta_two) * grad * grad
    fix_first = 1.0 - jnp.power(jnp.float32(beta_one), count)
    fix_second = 1.0 - jnp.power(jnp.float32(beta_two), count)
    master_new = master - learn_rate * (first_new / fix_first) / (jnp.sqrt(second_new / fix_second) + adam_eps)
    return (master_new, first_new, second_new)

def one_section(pack, count):
    acts, value_grad, loss_weight, value_weight, down_master, down_first, down_second, up_master, up_first, up_second = pack
    weight_f = loss_weight.astype(jnp.float32)
    share = weight_f / jnp.sum(weight_f)
    scaled = (value_grad.astype(jnp.float32) * share[:, None]).astype(jnp.bfloat16)
    down_cur = down_master.astype(jnp.bfloat16)
    up_cur = up_master.astype(jnp.bfloat16)
    mid = (adapter_scale * jnp.dot(scaled, up_cur.T, preferred_element_type=jnp.float32)).astype(jnp.bfloat16)
    low = jnp.dot(acts, down_cur, preferred_element_type=jnp.float32).astype(jnp.bfloat16)
    grad_down = jnp.dot(acts.T, mid, preferred_element_type=jnp.float32)
    grad_up = adapter_scale * jnp.dot(low.T, scaled, preferred_element_type=jnp.float32)
    input_grad = (jnp.dot(scaled, value_weight.T, preferred_element_type=jnp.float32) + jnp.dot(mid, down_cur.T, preferred_element_type=jnp.float32)).astype(jnp.bfloat16)
    down_new, down_first_new, down_second_new = adam_update(down_master, down_first, down_second, grad_down, count)
    up_new, up_first_new, up_second_new = adam_update(up_master, up_first, up_second, grad_up, count)
    low_new = jnp.dot(acts, down_new.astype(jnp.bfloat16), preferred_element_type=jnp.float32).astype(jnp.bfloat16)
    refreshed = (adapter_scale * jnp.dot(low_new, up_new.astype(jnp.bfloat16), preferred_element_type=jnp.float32)).astype(jnp.bfloat16)
    return (input_grad, refreshed, down_new, down_first_new, down_second_new, up_new, up_first_new, up_second_new)

def reference(acts, value_grad, loss_weight, value_weight, down_master, down_first, down_second, up_master, up_first, up_second, step_count):
    count = step_count.astype(jnp.float32)[0]
    pack = (acts, value_grad, loss_weight, value_weight, down_master, down_first, down_second, up_master, up_first, up_second)
    results = lax.map(lambda item: one_section(item, count), pack)
    input_grads = results[0]
    upstream_grad = jnp.concatenate([input_grads[1:], jnp.zeros_like(input_grads[:1])], axis=0)
    return (upstream_grad, results[1], results[2], results[3], results[4], results[5], results[6], results[7])
```

```python
import jax
import jax.numpy as jnp
from jax import lax
from jax.sharding import Mesh, PartitionSpec as P

adapter_scale = 2.0
beta_one = 0.9
beta_two = 0.999
learn_rate = 0.05
adam_eps = 1e-08

LANES = 128
bf16 = jnp.bfloat16
f32 = jnp.float32


def adam_update(master, first, second, grad, count):
    first_new = beta_one * first + (1.0 - beta_one) * grad
    second_new = beta_two * second + (1.0 - beta_two) * grad * grad
    fix_first = 1.0 - jnp.power(jnp.float32(beta_one), count)
    fix_second = 1.0 - jnp.power(jnp.float32(beta_two), count)
    master_new = master - learn_rate * (first_new / fix_first) / (
        jnp.sqrt(second_new / fix_second) + adam_eps
    )
    return (master_new, first_new, second_new)


def from_next_section(array):
    size = lax.axis_size("section")
    return lax.ppermute(array, "section", [(i, i - 1) for i in range(1, size)])


def gather_blocks(block):
    got = lax.all_gather(block, "z")
    got = lax.all_gather(got, "yl")
    return lax.all_gather(got, "core")


def reduce_blocks(blocks):
    got = lax.all_to_all(blocks, "core", 0, 0)
    kept = got[0] + got[1]
    got = lax.all_to_all(kept.astype(bf16), "yl", 0, 0)
    kept = got[0].astype(f32) + got[1].astype(f32)
    got = lax.all_to_all(kept.astype(bf16), "z", 0, 0)
    return jnp.sum(got.astype(f32), axis=0)


def pad_rows(parts, rows):
    have = sum(p.shape[0] for p in parts)
    if have < rows:
        parts = parts + [jnp.zeros((rows - have, LANES), parts[0].dtype)]
    return jnp.concatenate(parts, axis=0)


def per_device(
    acts,
    value_grad,
    loss_weight,
    value_weight,
    down_master,
    down_first,
    down_second,
    up_master,
    up_first,
    up_second,
    step_count,
):
    tokens, width = acts.shape[1:]
    features = value_grad.shape[2]
    rank = down_master.shape[2]
    up_rows = features // LANES
    rows = -(-(rank + up_rows + 2) // 8) * 8
    acts = acts[0]
    down_cur = down_master[0].T.astype(bf16)
    up_cur = up_master[0].astype(bf16).reshape(up_rows, LANES)

    weights = jnp.concatenate([value_weight[0].T, down_cur], axis=0)
    weights = from_next_section(weights)
    weights_all = lax.all_gather(weights, ("z", "yl", "core"))

    part = jnp.sum(loss_weight)
    high, low_bits = part // 128, part % 128
    count_rows = jnp.stack([high, low_bits]).astype(bf16)[:, None] * jnp.ones((1, LANES), bf16)
    got = gather_blocks(pad_rows([down_cur, up_cur, count_rows], rows))
    got = jnp.transpose(got, (2, 1, 0, 3, 4)).reshape(-1, rows, LANES)
    counts = got[:, rank + up_rows : rank + up_rows + 2, 0].astype(f32)
    total = jnp.sum(counts[:, 0] * 128.0 + counts[:, 1])
    share = loss_weight[0].astype(f32) / total
    scaled = (value_grad[0].astype(f32) * share[:, None]).astype(bf16)
    down_all = jnp.transpose(got[:, :rank], (1, 0, 2)).reshape(rank, width)
    up_all = got[:, rank : rank + up_rows].reshape(rank, features)

    mid = (adapter_scale * jnp.einsum("tk,rk->tr", scaled, up_all, preferred_element_type=f32)).astype(bf16)
    low = jnp.einsum("td,rd->tr", acts, down_all, preferred_element_type=f32).astype(bf16)
    next_rows = from_next_section(jnp.concatenate([scaled, mid], axis=1))
    grad_down = jnp.einsum("tr,td->rd", mid, acts, preferred_element_type=f32)
    grad_up = adapter_scale * jnp.einsum("tr,tk->rk", low, scaled, preferred_element_type=f32)

    z = lax.axis_size("z")
    grad = jnp.concatenate(
        [
            jnp.transpose(grad_down.reshape(rank, -1, LANES), (1, 0, 2)),
            grad_up.reshape(-1, up_rows, LANES),
            jnp.zeros((4 * z, rows - rank - up_rows, LANES), f32),
        ],
        axis=1,
    )
    grad = jnp.transpose(grad.reshape(z, 2, 2, rows, LANES), (2, 1, 0, 3, 4))
    grad = reduce_blocks(grad)

    count = step_count.astype(f32)[0]
    down_new, down_first_new, down_second_new = adam_update(
        down_master[0].T, down_first[0].T, down_second[0].T, grad[:rank], count
    )
    up_new, up_first_new, up_second_new = adam_update(
        up_master[0], up_first[0], up_second[0], grad[rank : rank + up_rows].reshape(1, features), count
    )
    got = gather_blocks(
        pad_rows([down_new.astype(bf16), up_new.astype(bf16).reshape(up_rows, LANES)], rows)
    )
    got = jnp.transpose(got, (2, 1, 0, 3, 4)).reshape(-1, rows, LANES)
    down_next = jnp.transpose(got[:, :rank], (1, 0, 2)).reshape(rank, width)
    up_next = got[:, rank : rank + up_rows].reshape(rank, features)
    low_new = jnp.einsum("td,rd->tr", acts, down_next, preferred_element_type=f32).astype(bf16)
    refreshed = (
        adapter_scale * jnp.einsum("tr,rk->tk", low_new, up_next, preferred_element_type=f32)
    ).astype(bf16)

    upstream = jnp.einsum("tk,bkd->tbd", next_rows, weights_all, preferred_element_type=f32)
    upstream = upstream.astype(bf16).reshape(tokens, width)
    return (
        upstream[None],
        refreshed[None],
        down_new.T[None],
        down_first_new.T[None],
        down_second_new.T[None],
        up_new[None],
        up_first_new[None],
        up_second_new[None],
    )


def solution(mesh):
    sections, dp = mesh.devices.shape
    staged = Mesh(mesh.devices.reshape(sections, dp // 4, 2, 2), ("section", "z", "yl", "core"))
    split = P("section", ("z", "yl", "core"))
    return jax.shard_map(
        per_device,
        mesh=staged,
        in_specs=(split,) * 10 + (P(),),
        out_specs=(split,) * 8,
        check_vma=False,
    )
```

```python
import functools
import jax
import jax.numpy as jnp
from jax import lax
from jax.experimental import pallas as pl
from jax.experimental.pallas import tpu as pltpu
from jax.sharding import Mesh, PartitionSpec as P

adapter_scale = 2.0
beta_one = 0.9
beta_two = 0.999
learn_rate = 0.05
adam_eps = 1e-08

LANES = 128
EXTRA = 8
bf16 = jnp.bfloat16
f32 = jnp.float32
VMEM_BYTES = 20 * 1024 * 1024


def adam_update(master, first, second, grad, count):
    first_new = beta_one * first + (1.0 - beta_one) * grad
    second_new = beta_two * second + (1.0 - beta_two) * grad * grad
    fix_first = 1.0 - jnp.power(jnp.float32(beta_one), count)
    fix_second = 1.0 - jnp.power(jnp.float32(beta_two), count)
    master_new = master - learn_rate * (first_new / fix_first) / (
        jnp.sqrt(second_new / fix_second) + adam_eps
    )
    return (master_new, first_new, second_new)


def swap(array, axis):
    return lax.ppermute(array, axis, [(0, 1), (1, 0)])


def after(value, *others):
    return lax.optimization_barrier((value,) + others)


def spread(block):
    z = lax.axis_size("z")
    return lax.all_to_all(jnp.broadcast_to(block[None], (z,) + block.shape), "z", 0, 0)


def pad_rows(parts, rows):
    have = sum(p.shape[0] for p in parts)
    if have < rows:
        parts = parts + [jnp.zeros((rows - have, LANES), parts[0].dtype)]
    return jnp.concatenate(parts, axis=0)


def nn(a, b):
    return jnp.dot(a, b, preferred_element_type=f32)


def nt(a, b):
    return lax.dot_general(a, b, (((1,), (1,)), ((), ())), preferred_element_type=f32)


def target_of(q, core, z, rank, up_rows):
    j = q % EXTRA
    block = q // EXTRA
    half = block // (2 * z)
    yl = (block // z) % 2
    row = (block % z) * 4 + yl * 2 + jnp.where(half == 0, core, 1 - core)
    return jnp.where(j < up_rows, j * rank + row, jnp.where(j < up_rows + 2, up_rows * rank + j - up_rows, -1))


def unpack(core, halves, down, extra, rank):
    z = halves[0].shape[1]
    for half, ref in enumerate(halves):
        owner = core if half == 0 else 1 - core
        for yl in range(2):
            for i in range(z):
                at = pl.multiple_of((i * 2 + yl) * 2 * LANES + owner * LANES, LANES)
                down[:, pl.ds(at, LANES)] = ref[yl, i, :rank, :]
                row = ((half * 2 + yl) * z + i) * EXTRA
                extra[row : row + EXTRA, :] = ref[yl, i, rank:, :]


def up_rows_of(core, extra, z, rank, up_rows):
    places = up_rows * rank + 16
    shape = (places, extra.shape[0])
    q = lax.broadcasted_iota(jnp.int32, (1, shape[1]), 1)
    pick = lax.broadcasted_iota(jnp.int32, shape, 0) == target_of(q, core, z, rank, up_rows)
    found = nn(pick.astype(f32).astype(bf16), extra[...])
    up = jnp.concatenate(
        [found[k * rank : (k + 1) * rank].astype(bf16) for k in range(up_rows)], axis=1
    )
    return up, found[up_rows * rank :]


def backward_kernel(
    place, mine, other, acts, value_grad, loss_weight, keep, send, rows_out, down, extra
):
    core, yl_here = place[0], place[1]
    z = mine.shape[1]
    rank = down.shape[0]
    tokens, features = value_grad.shape
    up_rows = features // LANES
    unpack(core, (mine, other), down, extra, rank)
    up, counts = up_rows_of(core, extra, z, rank, up_rows)
    total = counts[0:1, :1] * 128.0 + counts[1:2, :1]
    weight = jnp.broadcast_to(loss_weight[...].astype(f32), (tokens, tokens))
    square = (tokens, tokens)
    diagonal = lax.broadcasted_iota(jnp.int32, square, 0) == lax.broadcasted_iota(jnp.int32, square, 1)
    share = jnp.sum(jnp.where(diagonal, weight, 0.0), axis=1, keepdims=True) / total
    scaled = (value_grad[...].astype(f32) * share).astype(bf16)
    rows_out[:, :features] = scaled
    rows_out[:, features:] = (adapter_scale * nt(scaled, up)).astype(bf16)
    mid_t = (adapter_scale * nt(up, scaled)).astype(bf16)
    low_t = nt(down[...], acts[...]).astype(bf16)

    shape = (extra.shape[0], up_rows * rank)
    q = lax.broadcasted_iota(jnp.int32, (shape[0], 1), 0)
    put = lax.broadcasted_iota(jnp.int32, shape, 1) == target_of(q, core, z, rank, up_rows)
    put = put.astype(f32).astype(bf16)
    up_grad = jnp.zeros((shape[0], LANES), f32)
    for k in range(up_rows):
        low_k = nn(put[:, k * rank : (k + 1) * rank], low_t).astype(bf16)
        up_grad = up_grad + nn(low_k, scaled[:, k * LANES : (k + 1) * LANES])
    up_grad = adapter_scale * up_grad

    for yl in range(2):
        to = jnp.bitwise_xor(yl, yl_here)
        for i in range(z):
            at = (i * 2 + yl) * 2 * LANES
            grad = nn(mid_t, acts[:, at : at + 2 * LANES])
            first, second = grad[:, :LANES], grad[:, LANES:]
            row = (yl * z + i) * EXTRA
            keep[to, i, :rank, :] = jnp.where(core == 0, first, second)
            keep[to, i, rank:, :] = up_grad[row : row + EXTRA]
            row = ((2 + yl) * z + i) * EXTRA
            send[to, i, :rank, :] = jnp.where(core == 0, second, first).astype(bf16)
            send[to, i, rank:, :] = up_grad[row : row + EXTRA].astype(bf16)


def refresh_kernel(place, mine, other, acts, out, down, extra):
    core = place[0]
    rank = down.shape[0]
    unpack(core, (mine, other), down, extra, rank)
    up, _ = up_rows_of(core, extra, mine.shape[1], rank, out.shape[1] // LANES)
    low = nt(acts[...], down[...]).astype(bf16)
    out[...] = (adapter_scale * nn(low, up)).astype(bf16)


def input_grad_kernel(place, rows, mine, other, out):
    core = place[0]
    for i in range(mine.shape[0]):
        w_mine, w_other = mine[i], other[i]
        pair = jnp.concatenate(
            [jnp.where(core == 0, w_mine, w_other), jnp.where(core == 0, w_other, w_mine)], axis=1
        )
        out[:, i * 2 * LANES : (i + 1) * 2 * LANES] = nn(rows[...], pair).astype(bf16)


def whole(n):
    return [pl.BlockSpec(memory_space=pltpu.VMEM)] * n


SCALARS = pl.BlockSpec(memory_space=pltpu.SMEM)


def per_device(
    acts,
    value_grad,
    loss_weight,
    value_weight,
    down_master,
    down_first,
    down_second,
    up_master,
    up_first,
    up_second,
    step_count,
):
    tokens, width = acts.shape[1:]
    features = value_grad.shape[2]
    rank = down_master.shape[2]
    up_rows = features // LANES
    rows = rank + EXTRA
    z, sections = lax.axis_size("z"), lax.axis_size("section")
    place = jnp.stack([lax.axis_index("core"), lax.axis_index("yl")]).astype(jnp.int32)
    params = pltpu.CompilerParams(vmem_limit_bytes=VMEM_BYTES)
    acts = acts[0]
    down_cur = down_master[0].T.astype(bf16)
    up_cur = up_master[0].astype(bf16).reshape(up_rows, LANES)

    weights = jnp.concatenate([value_weight[0].T, down_cur], axis=0)

    def from_next(flip):
        return [
            (s * 2 + (yl ^ flip), (s - 1) * 2 + yl) for s in range(1, sections) for yl in range(2)
        ]

    same = lax.ppermute(weights, ("section", "yl"), from_next(0))
    flipped = lax.ppermute(weights, ("section", "yl"), from_next(1))

    part = jnp.sum(loss_weight)
    count_rows = jnp.stack([part // 128, part % 128]).astype(bf16)[:, None] * jnp.ones((1, LANES), bf16)
    got = spread(pad_rows([down_cur, up_cur, count_rows], rows))
    got, same, flipped = after(got, same, flipped)
    even = lax.axis_index("yl") == 0
    weights = jnp.stack([jnp.where(even, same, flipped), jnp.where(even, flipped, same)])
    weights_mine = lax.all_gather(weights, "z").reshape(2 * z, features + rank, LANES)

    got = lax.all_gather(got, "yl")
    keep, send, next_rows = pl.pallas_call(
        backward_kernel,
        out_shape=(
            jax.ShapeDtypeStruct((2, z, rows, LANES), f32),
            jax.ShapeDtypeStruct((2, z, rows, LANES), bf16),
            jax.ShapeDtypeStruct((tokens, features + rank), bf16),
        ),
        in_specs=[SCALARS] + whole(5),
        out_specs=tuple(whole(3)),
        scratch_shapes=[
            pltpu.VMEM((rank, width), bf16),
            pltpu.VMEM((4 * z * EXTRA, LANES), bf16),
        ],
        compiler_params=params,
        name="backward",
    )(place, got, swap(got, "core"), acts, value_grad[0], loss_weight)
    next_rows = lax.ppermute(next_rows, "section", [(s, s - 1) for s in range(1, sections)])

    kept = keep + swap(send, "core").astype(f32)
    kept = kept[0] + swap(kept[1].astype(bf16), "yl").astype(f32)
    grad = jnp.sum(lax.all_to_all(kept.astype(bf16), "z", 0, 0).astype(f32), axis=0)

    count = step_count.astype(f32)[0]
    down_new, down_first_new, down_second_new = adam_update(
        down_master[0].T, down_first[0].T, down_second[0].T, grad[:rank], count
    )
    up_new, up_first_new, up_second_new = adam_update(
        up_master[0], up_first[0], up_second[0], grad[rank : rank + up_rows].reshape(1, features), count
    )
    got = spread(pad_rows([down_new.astype(bf16), up_new.astype(bf16).reshape(up_rows, LANES)], rows))
    got, weights_mine = after(got, weights_mine)
    weights_other = swap(weights_mine, "core")
    got = lax.all_gather(got, "yl")
    refreshed = pl.pallas_call(
        refresh_kernel,
        out_shape=jax.ShapeDtypeStruct((tokens, features), bf16),
        in_specs=[SCALARS] + whole(3),
        out_specs=whole(1)[0],
        scratch_shapes=[
            pltpu.VMEM((rank, width), bf16),
            pltpu.VMEM((4 * z * EXTRA, LANES), bf16),
        ],
        compiler_params=params,
        name="refresh",
    )(place, got, swap(got, "core"), acts)

    chunk = min(4, 2 * z)
    w_spec = pl.BlockSpec((chunk, features + rank, LANES), lambda i: (i, 0, 0))
    upstream = pl.pallas_call(
        input_grad_kernel,
        out_shape=jax.ShapeDtypeStruct((tokens, width), bf16),
        grid=(2 * z // chunk,),
        in_specs=[
            SCALARS,
            pl.BlockSpec((tokens, features + rank), lambda i: (0, 0)),
            w_spec,
            w_spec,
        ],
        out_specs=pl.BlockSpec((tokens, chunk * 2 * LANES), lambda i: (0, i)),
        compiler_params=params,
        name="input_grad",
    )(place, next_rows, weights_mine, weights_other)
    return (
        upstream[None],
        refreshed[None],
        down_new.T[None],
        down_first_new.T[None],
        down_second_new.T[None],
        up_new[None],
        up_first_new[None],
        up_second_new[None],
    )


def solution(mesh):
    sections, dp = mesh.devices.shape
    staged = Mesh(mesh.devices.reshape(sections, dp // 4, 2, 2), ("section", "z", "yl", "core"))
    split = P("section", ("z", "yl", "core"))
    return jax.shard_map(
        per_device,
        mesh=staged,
        in_specs=(split,) * 10 + (P(),),
        out_specs=(split,) * 8,
        check_vma=False,
    )
```

```python
import jax
import jax.numpy as jnp
from jax import lax
from jax.experimental import pallas as pl
from jax.experimental.pallas import tpu as pltpu
from jax.sharding import Mesh, PartitionSpec as P

adapter_scale = 2.0
beta_one = 0.9
beta_two = 0.999
learn_rate = 0.05
adam_eps = 1e-08

LANES = 128
EXTRA = 8
bf16 = jnp.bfloat16
f32 = jnp.float32
VMEM_BYTES = 20 * 1024 * 1024


def adam_update(master, first, second, grad, count):
    first_new = beta_one * first + (1.0 - beta_one) * grad
    second_new = beta_two * second + (1.0 - beta_two) * grad * grad
    fix_first = 1.0 - jnp.power(jnp.float32(beta_one), count)
    fix_second = 1.0 - jnp.power(jnp.float32(beta_two), count)
    master_new = master - learn_rate * (first_new / fix_first) / (
        jnp.sqrt(second_new / fix_second) + adam_eps
    )
    return (master_new, first_new, second_new)


def swap(array, axis):
    return lax.ppermute(array, axis, [(0, 1), (1, 0)])


def quarters(got, beside=None):
    got_yl = swap(got, "yl")
    got_yl, beside = after(got_yl, beside)
    return (got, got_yl, swap(got, "core"), swap(got_yl, "core")), beside


def after(value, *others):
    return lax.optimization_barrier((value,) + others)


def spread(copies):
    return lax.all_to_all(copies, "z", 0, 0)


def pad_rows(parts, rows):
    have = sum(p.shape[0] for p in parts)
    if have < rows:
        parts = parts + [jnp.zeros((rows - have, LANES), parts[0].dtype)]
    return jnp.concatenate(parts, axis=0)


def nn(a, b):
    return jnp.dot(a, b, preferred_element_type=f32)


def nt(a, b):
    return lax.dot_general(a, b, (((1,), (1,)), ((), ())), preferred_element_type=f32)


def target_of(q, core, yl, z, rank, up_rows):
    j = q % EXTRA
    block = q // EXTRA
    of_core = jnp.where(block // (2 * z) == 0, core, 1 - core)
    of_yl = jnp.where((block // z) % 2 == 0, yl, 1 - yl)
    row = (block % z) * 4 + of_yl * 2 + of_core
    return jnp.where(j < up_rows, j * rank + row, jnp.where(j < up_rows + 2, up_rows * rank + j - up_rows, -1))


def unpack(core, yl, quarters, down, extra, rank):
    z = quarters[0].shape[0]
    for quarter, ref in enumerate(quarters):
        of_core = core if quarter < 2 else 1 - core
        of_yl = yl if quarter % 2 == 0 else 1 - yl
        offset = (of_yl * 2 + of_core) * LANES
        for i in range(z):
            at = pl.multiple_of(i * 4 * LANES + offset, LANES)
            down[:, pl.ds(at, LANES)] = ref[i, :rank, :]
            row = (quarter * z + i) * EXTRA
            extra[row : row + EXTRA, :] = ref[i, rank:, :]


def up_rows_of(core, yl, extra, z, rank, up_rows):
    places = up_rows * rank + 16
    shape = (places, extra.shape[0])
    q = lax.broadcasted_iota(jnp.int32, (1, shape[1]), 1)
    pick = lax.broadcasted_iota(jnp.int32, shape, 0) == target_of(q, core, yl, z, rank, up_rows)
    found = nn(pick.astype(f32).astype(bf16), extra[...])
    up = jnp.concatenate(
        [found[k * rank : (k + 1) * rank].astype(bf16) for k in range(up_rows)], axis=1
    )
    return up, found[up_rows * rank :]


def prepare_kernel(down_master, up_master, loss_weight, value_weight, copies, weights):
    rank = down_master.shape[0]
    features = up_master.shape[1]
    down = down_master[...].astype(bf16)
    count = jnp.sum(loss_weight[...].astype(f32), axis=1, keepdims=True)
    high = jnp.floor(count / 128.0)
    parts = [up_master[:, at : at + LANES] for at in range(0, features, LANES)]
    parts += [jnp.broadcast_to(c, (1, LANES)) for c in (high, count - 128.0 * high)]
    parts.append(jnp.zeros((EXTRA - len(parts), LANES), f32))
    extra = jnp.concatenate(parts, axis=0).astype(bf16)
    for i in range(copies.shape[0]):
        copies[i, :rank, :] = down
        copies[i, rank:, :] = extra
    weights[:features, :] = value_weight[...].astype(f32).T.astype(bf16)
    weights[features:, :] = down


def backward_kernel(
    place, q0, q1, q2, q3, acts, value_grad, loss_weight, keep, send, rows_out, down, extra
):
    core, yl = place[0], place[1]
    z = q0.shape[0]
    rank = down.shape[0]
    tokens, features = value_grad.shape
    up_rows = features // LANES
    unpack(core, yl, (q0, q1, q2, q3), down, extra, rank)
    up, counts = up_rows_of(core, yl, extra, z, rank, up_rows)
    total = counts[0:1, :1] * 128.0 + counts[1:2, :1]
    weight = jnp.broadcast_to(loss_weight[...].astype(f32), (tokens, tokens))
    square = (tokens, tokens)
    diagonal = lax.broadcasted_iota(jnp.int32, square, 0) == lax.broadcasted_iota(jnp.int32, square, 1)
    share = jnp.sum(jnp.where(diagonal, weight, 0.0), axis=1, keepdims=True) / total
    scaled = (value_grad[...].astype(f32) * share).astype(bf16)
    rows_out[:, :features] = scaled
    rows_out[:, features:] = (adapter_scale * nt(scaled, up)).astype(bf16)
    mid_t = (adapter_scale * nt(up, scaled)).astype(bf16)
    low_t = nt(down[...], acts[...]).astype(bf16)

    shape = (extra.shape[0], up_rows * rank)
    q = lax.broadcasted_iota(jnp.int32, (shape[0], 1), 0)
    put = lax.broadcasted_iota(jnp.int32, shape, 1) == target_of(q, core, yl, z, rank, up_rows)
    put = put.astype(f32).astype(bf16)
    up_grad = jnp.zeros((shape[0], LANES), f32)
    for k in range(up_rows):
        low_k = nn(put[:, k * rank : (k + 1) * rank], low_t).astype(bf16)
        up_grad = up_grad + nn(low_k, scaled[:, k * LANES : (k + 1) * LANES])
    up_grad = adapter_scale * up_grad

    for half in range(2):
        of_yl = yl if half == 0 else 1 - yl
        for i in range(z):
            at = pl.multiple_of(i * 4 * LANES + of_yl * 2 * LANES, 2 * LANES)
            grad = nn(mid_t, acts[:, pl.ds(at, 2 * LANES)])
            first, second = grad[:, :LANES], grad[:, LANES:]
            row = (half * z + i) * EXTRA
            keep[half, i, :rank, :] = jnp.where(core == 0, first, second)
            keep[half, i, rank:, :] = up_grad[row : row + EXTRA]
            row = ((2 + half) * z + i) * EXTRA
            send[half, i, :rank, :] = jnp.where(core == 0, second, first).astype(bf16)
            send[half, i, rank:, :] = up_grad[row : row + EXTRA].astype(bf16)


def refresh_kernel(place, q0, q1, q2, q3, acts, out, down, extra):
    core, yl = place[0], place[1]
    rank = down.shape[0]
    unpack(core, yl, (q0, q1, q2, q3), down, extra, rank)
    up, _ = up_rows_of(core, yl, extra, q0.shape[0], rank, out.shape[1] // LANES)
    low = nt(acts[...], down[...]).astype(bf16)
    out[...] = (adapter_scale * nn(low, up)).astype(bf16)


def side_by_side(blocks):
    return jnp.concatenate([blocks[i] for i in range(blocks.shape[0])], axis=1)


def own_columns_kernel(rows, weights, out):
    out[...] = nn(rows[...], side_by_side(weights)).astype(bf16)


def all_columns_kernel(place, rows, weights, mine, out):
    core = place[0]
    other = nn(rows[...], side_by_side(weights)).astype(bf16)
    for i in range(weights.shape[0]):
        at = i * 2 * LANES
        a, b = mine[:, i * LANES : (i + 1) * LANES], other[:, i * LANES : (i + 1) * LANES]
        out[:, at : at + LANES] = jnp.where(core == 0, a, b)
        out[:, at + LANES : at + 2 * LANES] = jnp.where(core == 0, b, a)


def whole(n):
    return [pl.BlockSpec(memory_space=pltpu.VMEM)] * n


SCALARS = pl.BlockSpec(memory_space=pltpu.SMEM)


def per_device(
    acts,
    value_grad,
    loss_weight,
    value_weight,
    down_master,
    down_first,
    down_second,
    up_master,
    up_first,
    up_second,
    step_count,
):
    tokens, width = acts.shape[1:]
    features = value_grad.shape[2]
    rank = down_master.shape[2]
    up_rows = features // LANES
    rows = rank + EXTRA
    z, sections = lax.axis_size("z"), lax.axis_size("section")
    place = jnp.stack([lax.axis_index("core"), lax.axis_index("yl")]).astype(jnp.int32)
    params = pltpu.CompilerParams(vmem_limit_bytes=VMEM_BYTES)
    acts = acts[0]
    copies, weights = pl.pallas_call(
        prepare_kernel,
        out_shape=(
            jax.ShapeDtypeStruct((z, rows, LANES), bf16),
            jax.ShapeDtypeStruct((features + rank, LANES), bf16),
        ),
        in_specs=whole(4),
        out_specs=tuple(whole(2)),
        compiler_params=params,
        name="prepare",
    )(down_master[0].T, up_master[0], loss_weight, value_weight[0])

    def from_next(flip):
        return [
            (s * 2 + (yl ^ flip), (s - 1) * 2 + yl) for s in range(1, sections) for yl in range(2)
        ]

    same = lax.ppermute(weights, ("section", "yl"), from_next(0))
    flipped = lax.ppermute(weights, ("section", "yl"), from_next(1))

    got = spread(copies)
    got, same, flipped = after(got, same, flipped)
    even = lax.axis_index("yl") == 0
    weights = jnp.stack([jnp.where(even, same, flipped), jnp.where(even, flipped, same)])
    weights_mine = lax.all_gather(weights, "z").reshape(2 * z, features + rank, LANES)

    blocks, _ = quarters(got)
    keep, send, next_rows = pl.pallas_call(
        backward_kernel,
        out_shape=(
            jax.ShapeDtypeStruct((2, z, rows, LANES), f32),
            jax.ShapeDtypeStruct((2, z, rows, LANES), bf16),
            jax.ShapeDtypeStruct((tokens, features + rank), bf16),
        ),
        in_specs=[SCALARS] + whole(7),
        out_specs=tuple(whole(3)),
        scratch_shapes=[
            pltpu.VMEM((rank, width), bf16),
            pltpu.VMEM((4 * z * EXTRA, LANES), bf16),
        ],
        compiler_params=params,
        name="backward",
    )(place, *blocks, acts, value_grad[0], loss_weight)
    next_rows = lax.ppermute(next_rows, "section", [(s, s - 1) for s in range(1, sections)])

    kept = keep + swap(send, "core").astype(f32)
    kept = kept[0] + swap(kept[1].astype(bf16), "yl").astype(f32)
    parts, next_rows = after(lax.all_to_all(kept.astype(bf16), "z", 0, 0), next_rows)
    grad = jnp.sum(parts.astype(f32), axis=0)

    count = step_count.astype(f32)[0]
    down_new, down_first_new, down_second_new = adam_update(
        down_master[0].T, down_first[0].T, down_second[0].T, grad[:rank], count
    )
    up_new, up_first_new, up_second_new = adam_update(
        up_master[0], up_first[0], up_second[0], grad[rank : rank + up_rows].reshape(1, features), count
    )
    block = pad_rows([down_new.astype(bf16), up_new.astype(bf16).reshape(up_rows, LANES)], rows)
    got = spread(jnp.broadcast_to(block[None], (z, rows, LANES)))
    got, weights_mine = after(got, weights_mine)
    weights_other = swap(weights_mine, "core")
    chunk = min(4, 2 * z)
    rows_spec = pl.BlockSpec((tokens, features + rank), lambda i: (0, 0))
    w_spec = pl.BlockSpec((chunk, features + rank, LANES), lambda i: (i, 0, 0))
    half_spec = pl.BlockSpec((tokens, chunk * LANES), lambda i: (0, i))
    own_columns = pl.pallas_call(
        own_columns_kernel,
        out_shape=jax.ShapeDtypeStruct((tokens, width // 2), bf16),
        grid=(2 * z // chunk,),
        in_specs=[rows_spec, w_spec],
        out_specs=half_spec,
        compiler_params=pltpu.CompilerParams(vmem_limit_bytes=56 * 1024 * 1024),
        cost_estimate=pl.CostEstimate(
            flops=tokens * (features + rank) * width,
            bytes_accessed=(features + rank) * width + tokens * width,
            transcendentals=0,
        ),
        name="own_columns",
    )(next_rows, weights_mine)
    blocks, own_columns = quarters(got, own_columns)
    refreshed = pl.pallas_call(
        refresh_kernel,
        out_shape=jax.ShapeDtypeStruct((tokens, features), bf16),
        in_specs=[SCALARS] + whole(5),
        out_specs=whole(1)[0],
        scratch_shapes=[
            pltpu.VMEM((rank, width), bf16),
            pltpu.VMEM((4 * z * EXTRA, LANES), bf16),
        ],
        compiler_params=params,
        name="refresh",
    )(place, *blocks, acts)

    upstream = pl.pallas_call(
        all_columns_kernel,
        out_shape=jax.ShapeDtypeStruct((tokens, width), bf16),
        grid=(2 * z // chunk,),
        in_specs=[SCALARS, rows_spec, w_spec, half_spec],
        out_specs=pl.BlockSpec((tokens, chunk * 2 * LANES), lambda i: (0, i)),
        compiler_params=params,
        name="all_columns",
    )(place, next_rows, weights_other, own_columns)
    return (
        upstream[None],
        refreshed[None],
        down_new.T[None],
        down_first_new.T[None],
        down_second_new.T[None],
        up_new[None],
        up_first_new[None],
        up_second_new[None],
    )


def solution(mesh):
    sections, dp = mesh.devices.shape
    staged = Mesh(mesh.devices.reshape(sections, dp // 4, 2, 2), ("section", "z", "yl", "core"))
    split = P("section", ("z", "yl", "core"))
    return jax.shard_map(
        per_device,
        mesh=staged,
        in_specs=(split,) * 10 + (P(),),
        out_specs=(split,) * 8,
        check_vma=False,
    )
```

```python
import jax
import jax.numpy as jnp
from jax import lax
from jax.experimental import pallas as pl
from jax.experimental.pallas import tpu as pltpu
from jax.sharding import Mesh, PartitionSpec as P

adapter_scale = 2.0
beta_one = 0.9
beta_two = 0.999
learn_rate = 0.05
adam_eps = 1e-08

LANES = 128
EXTRA = 8
bf16 = jnp.bfloat16
f32 = jnp.float32
VMEM_BYTES = 20 * 1024 * 1024


def adam_update(master, first, second, grad, count):
    first_new = beta_one * first + (1.0 - beta_one) * grad
    second_new = beta_two * second + (1.0 - beta_two) * grad * grad
    fix_first = 1.0 - jnp.power(jnp.float32(beta_one), count)
    fix_second = 1.0 - jnp.power(jnp.float32(beta_two), count)
    master_new = master - learn_rate * (first_new / fix_first) / (
        jnp.sqrt(second_new / fix_second) + adam_eps
    )
    return (master_new, first_new, second_new)


def swap(array, axis):
    return lax.ppermute(array, axis, [(0, 1), (1, 0)])


def after(value, *others):
    return lax.optimization_barrier((value,) + others)


def spread(copies):
    return lax.all_to_all(copies, "z", 0, 0)


def pad_rows(parts, rows):
    have = sum(p.shape[0] for p in parts)
    if have < rows:
        parts = parts + [jnp.zeros((rows - have, LANES), parts[0].dtype)]
    return jnp.concatenate(parts, axis=0)


def nn(a, b):
    return jnp.dot(a, b, preferred_element_type=f32)


def nt(a, b):
    return lax.dot_general(a, b, (((1,), (1,)), ((), ())), preferred_element_type=f32)


def target_of(q, core, yl, z, rank, up_rows):
    j = q % EXTRA
    block = q // EXTRA
    of_core = jnp.where(block // (2 * z) == 0, core, 1 - core)
    of_yl = jnp.where((block // z) % 2 == 0, yl, 1 - yl)
    row = (block % z) * 4 + of_yl * 2 + of_core
    return jnp.where(j < up_rows, j * rank + row, jnp.where(j < up_rows + 2, up_rows * rank + j - up_rows, -1))


def unpack(core, yl, quarters, down, extra, rank):
    z = quarters[0].shape[0]
    for quarter, ref in enumerate(quarters):
        of_core = core if quarter < 2 else 1 - core
        of_yl = yl if quarter % 2 == 0 else 1 - yl
        offset = (of_yl * 2 + of_core) * LANES
        for i in range(z):
            at = pl.multiple_of(i * 4 * LANES + offset, LANES)
            down[:, pl.ds(at, LANES)] = ref[i, :rank, :]
            row = (quarter * z + i) * EXTRA
            extra[row : row + EXTRA, :] = ref[i, rank:, :]


def up_rows_of(core, yl, extra, z, rank, up_rows):
    places = up_rows * rank + 16
    shape = (places, extra.shape[0])
    q = lax.broadcasted_iota(jnp.int32, (1, shape[1]), 1)
    pick = lax.broadcasted_iota(jnp.int32, shape, 0) == target_of(q, core, yl, z, rank, up_rows)
    found = nn(pick.astype(f32).astype(bf16), extra[...])
    up = jnp.concatenate(
        [found[k * rank : (k + 1) * rank].astype(bf16) for k in range(up_rows)], axis=1
    )
    return up, found[up_rows * rank :]


def prepare_kernel(down_master, up_master, loss_weight, value_weight, copies, weights):
    rank = down_master.shape[0]
    features = up_master.shape[1]
    down = down_master[...].astype(bf16)
    count = jnp.sum(loss_weight[...].astype(f32), axis=1, keepdims=True)
    high = jnp.floor(count / 128.0)
    parts = [up_master[:, at : at + LANES] for at in range(0, features, LANES)]
    parts += [jnp.broadcast_to(c, (1, LANES)) for c in (high, count - 128.0 * high)]
    parts.append(jnp.zeros((EXTRA - len(parts), LANES), f32))
    extra = jnp.concatenate(parts, axis=0).astype(bf16)
    for i in range(copies.shape[0]):
        copies[i, :rank, :] = down
        copies[i, rank:, :] = extra
    weights[:features, :] = value_weight[...].astype(f32).T.astype(bf16)
    weights[features:, :] = down


def backward_kernel(
    place, q0, q1, q2, q3, acts, value_grad, loss_weight, keep, send, rows_out, down, extra
):
    core, yl = place[0], place[1]
    z = q0.shape[0]
    rank = down.shape[0]
    tokens, features = value_grad.shape
    up_rows = features // LANES
    unpack(core, yl, (q0, q1, q2, q3), down, extra, rank)
    up, counts = up_rows_of(core, yl, extra, z, rank, up_rows)
    total = counts[0:1, :1] * 128.0 + counts[1:2, :1]
    weight = jnp.broadcast_to(loss_weight[...].astype(f32), (tokens, tokens))
    square = (tokens, tokens)
    diagonal = lax.broadcasted_iota(jnp.int32, square, 0) == lax.broadcasted_iota(jnp.int32, square, 1)
    share = jnp.sum(jnp.where(diagonal, weight, 0.0), axis=1, keepdims=True) / total
    scaled = (value_grad[...].astype(f32) * share).astype(bf16)
    rows_out[:, :features] = scaled
    rows_out[:, features:] = (adapter_scale * nt(scaled, up)).astype(bf16)
    mid_t = (adapter_scale * nt(up, scaled)).astype(bf16)
    low_t = nt(down[...], acts[...]).astype(bf16)

    shape = (extra.shape[0], up_rows * rank)
    q = lax.broadcasted_iota(jnp.int32, (shape[0], 1), 0)
    put = lax.broadcasted_iota(jnp.int32, shape, 1) == target_of(q, core, yl, z, rank, up_rows)
    put = put.astype(f32).astype(bf16)
    up_grad = jnp.zeros((shape[0], LANES), f32)
    for k in range(up_rows):
        low_k = nn(put[:, k * rank : (k + 1) * rank], low_t).astype(bf16)
        up_grad = up_grad + nn(low_k, scaled[:, k * LANES : (k + 1) * LANES])
    up_grad = adapter_scale * up_grad

    for half in range(2):
        of_yl = yl if half == 0 else 1 - yl
        for i in range(z):
            at = pl.multiple_of(i * 4 * LANES + of_yl * 2 * LANES, 2 * LANES)
            grad = nn(mid_t, acts[:, pl.ds(at, 2 * LANES)])
            first, second = grad[:, :LANES], grad[:, LANES:]
            row = (half * z + i) * EXTRA
            keep[half, i, :rank, :] = jnp.where(core == 0, first, second)
            keep[half, i, rank:, :] = up_grad[row : row + EXTRA]
            row = ((2 + half) * z + i) * EXTRA
            send[half, i, :rank, :] = jnp.where(core == 0, second, first).astype(bf16)
            send[half, i, rank:, :] = up_grad[row : row + EXTRA].astype(bf16)


def refresh_kernel(place, q0, q1, q2, q3, acts, out, down, extra):
    core, yl = place[0], place[1]
    rank = down.shape[0]
    unpack(core, yl, (q0, q1, q2, q3), down, extra, rank)
    up, _ = up_rows_of(core, yl, extra, q0.shape[0], rank, out.shape[1] // LANES)
    low = nt(acts[...], down[...]).astype(bf16)
    out[...] = (adapter_scale * nn(low, up)).astype(bf16)


def pair_product(rows, weights, i):
    return nn(rows[...], jnp.concatenate([weights[i], weights[i + 1]], axis=1)).astype(bf16)


def own_columns_kernel(rows, weights, out):
    for i in range(0, weights.shape[0], 2):
        out[:, i * LANES : (i + 2) * LANES] = pair_product(rows, weights, i)


def all_columns_kernel(place, rows, weights, mine, out):
    core = place[0]
    for i in range(0, weights.shape[0], 2):
        other = pair_product(rows, weights, i)
        for j in range(2):
            a = mine[:, (i + j) * LANES : (i + j + 1) * LANES]
            b = other[:, j * LANES : (j + 1) * LANES]
            at = (i + j) * 2 * LANES
            out[:, at : at + LANES] = jnp.where(core == 0, a, b)
            out[:, at + LANES : at + 2 * LANES] = jnp.where(core == 0, b, a)


def whole(n):
    return [pl.BlockSpec(memory_space=pltpu.VMEM)] * n


SCALARS = pl.BlockSpec(memory_space=pltpu.SMEM)


def per_device(
    acts,
    value_grad,
    loss_weight,
    value_weight,
    down_master,
    down_first,
    down_second,
    up_master,
    up_first,
    up_second,
    step_count,
):
    tokens, width = acts.shape[1:]
    features = value_grad.shape[2]
    rank = down_master.shape[2]
    up_rows = features // LANES
    rows = rank + EXTRA
    z, sections = lax.axis_size("z"), lax.axis_size("section")
    place = jnp.stack([lax.axis_index("core"), lax.axis_index("yl")]).astype(jnp.int32)
    params = pltpu.CompilerParams(vmem_limit_bytes=VMEM_BYTES)
    acts = acts[0]
    copies, weights = pl.pallas_call(
        prepare_kernel,
        out_shape=(
            jax.ShapeDtypeStruct((z, rows, LANES), bf16),
            jax.ShapeDtypeStruct((features + rank, LANES), bf16),
        ),
        in_specs=whole(4),
        out_specs=tuple(whole(2)),
        compiler_params=pltpu.CompilerParams(vmem_limit_bytes=60 * 1024 * 1024),
        name="prepare",
    )(down_master[0].T, up_master[0], loss_weight, value_weight[0])

    def from_next(flip):
        return [
            (s * 2 + (yl ^ flip), (s - 1) * 2 + yl) for s in range(1, sections) for yl in range(2)
        ]

    same = lax.ppermute(weights, ("section", "yl"), from_next(0))
    flipped = lax.ppermute(weights, ("section", "yl"), from_next(1))

    even = lax.axis_index("yl") == 0
    weights = jnp.stack([jnp.where(even, same, flipped), jnp.where(even, flipped, same)])
    copies, weights = after(copies, weights)
    weights_mine = lax.all_gather(weights, "z").reshape(2 * z, features + rank, LANES)
    got = spread(copies)
    got_yl = swap(got, "yl")
    keep, send, next_rows = pl.pallas_call(
        backward_kernel,
        out_shape=(
            jax.ShapeDtypeStruct((2, z, rows, LANES), f32),
            jax.ShapeDtypeStruct((2, z, rows, LANES), bf16),
            jax.ShapeDtypeStruct((tokens, features + rank), bf16),
        ),
        in_specs=[SCALARS] + whole(7),
        out_specs=tuple(whole(3)),
        scratch_shapes=[
            pltpu.VMEM((rank, width), bf16),
            pltpu.VMEM((4 * z * EXTRA, LANES), bf16),
        ],
        compiler_params=params,
        name="backward",
    )(place, got, got_yl, swap(got, "core"), swap(got_yl, "core"), acts, value_grad[0], loss_weight)
    next_rows = lax.ppermute(next_rows, "section", [(s, s - 1) for s in range(1, sections)])

    kept = keep + swap(send, "core").astype(f32)
    kept = kept[0] + swap(kept[1].astype(bf16), "yl").astype(f32)
    parts, next_rows = after(lax.all_to_all(kept.astype(bf16), "z", 0, 0), next_rows)
    grad = jnp.sum(parts.astype(f32), axis=0)

    count = step_count.astype(f32)[0]
    down_new, down_first_new, down_second_new = adam_update(
        down_master[0].T, down_first[0].T, down_second[0].T, grad[:rank], count
    )
    up_new, up_first_new, up_second_new = adam_update(
        up_master[0], up_first[0], up_second[0], grad[rank : rank + up_rows].reshape(1, features), count
    )
    block = pad_rows([down_new.astype(bf16), up_new.astype(bf16).reshape(up_rows, LANES)], rows)
    got = spread(jnp.broadcast_to(block[None], (z, rows, LANES)))
    got, weights_mine = after(got, weights_mine)
    weights_other = swap(weights_mine, "core")
    chunk = min(4, 2 * z)
    product_cost = pl.CostEstimate(
        flops=tokens * (features + rank) * width,
        bytes_accessed=(features + rank) * width + tokens * width,
        transcendentals=0,
    )
    rows_spec = pl.BlockSpec((tokens, features + rank), lambda i: (0, 0))
    w_spec = pl.BlockSpec((chunk, features + rank, LANES), lambda i: (i, 0, 0))
    half_spec = pl.BlockSpec((tokens, chunk * LANES), lambda i: (0, i))
    own_columns = pl.pallas_call(
        own_columns_kernel,
        out_shape=jax.ShapeDtypeStruct((tokens, width // 2), bf16),
        grid=(2 * z // chunk,),
        in_specs=[rows_spec, w_spec],
        out_specs=half_spec,
        compiler_params=pltpu.CompilerParams(vmem_limit_bytes=56 * 1024 * 1024),
        cost_estimate=product_cost,
        name="own_columns",
    )(next_rows, weights_mine)
    got_yl, own_columns = after(swap(got, "yl"), own_columns)
    upstream = pl.pallas_call(
        all_columns_kernel,
        out_shape=jax.ShapeDtypeStruct((tokens, width), bf16),
        grid=(2 * z // chunk,),
        in_specs=[SCALARS, rows_spec, w_spec, half_spec],
        out_specs=pl.BlockSpec((tokens, chunk * 2 * LANES), lambda i: (0, i)),
        compiler_params=params,
        cost_estimate=product_cost,
        name="all_columns",
    )(place, next_rows, weights_other, own_columns)
    got_core, got_last = swap(got, "core"), swap(got_yl, "core")
    got_last, upstream = after(got_last, upstream)
    refreshed = pl.pallas_call(
        refresh_kernel,
        out_shape=jax.ShapeDtypeStruct((tokens, features), bf16),
        in_specs=[SCALARS] + whole(5),
        out_specs=whole(1)[0],
        scratch_shapes=[
            pltpu.VMEM((rank, width), bf16),
            pltpu.VMEM((4 * z * EXTRA, LANES), bf16),
        ],
        compiler_params=params,
        name="refresh",
    )(place, got, got_yl, got_core, got_last, acts)

    return (
        upstream[None],
        refreshed[None],
        down_new.T[None],
        down_first_new.T[None],
        down_second_new.T[None],
        up_new[None],
        up_first_new[None],
        up_second_new[None],
    )


def solution(mesh):
    sections, dp = mesh.devices.shape
    staged = Mesh(mesh.devices.reshape(sections, dp // 4, 2, 2), ("section", "z", "yl", "core"))
    split = P("section", ("z", "yl", "core"))
    return jax.shard_map(
        per_device,
        mesh=staged,
        in_specs=(split,) * 10 + (P(),),
        out_specs=(split,) * 8,
        check_vma=False,
    )
```

```python
import jax
import jax.numpy as jnp
from jax import lax
from jax.experimental import pallas as pl
from jax.experimental.pallas import tpu as pltpu
from jax.sharding import Mesh, PartitionSpec as P

adapter_scale = 2.0
beta_one = 0.9
beta_two = 0.999
learn_rate = 0.05
adam_eps = 1e-08

LANES = 128
EXTRA = 8
bf16 = jnp.bfloat16
f32 = jnp.float32
VMEM_BYTES = 20 * 1024 * 1024


def adam_update(master, first, second, grad, count):
    first_new = beta_one * first + (1.0 - beta_one) * grad
    second_new = beta_two * second + (1.0 - beta_two) * grad * grad
    fix_first = 1.0 - jnp.power(jnp.float32(beta_one), count)
    fix_second = 1.0 - jnp.power(jnp.float32(beta_two), count)
    master_new = master - learn_rate * (first_new / fix_first) / (
        jnp.sqrt(second_new / fix_second) + adam_eps
    )
    return (master_new, first_new, second_new)


def swap(array, axis):
    return lax.ppermute(array, axis, [(0, 1), (1, 0)])


def after(value, *others):
    return lax.optimization_barrier((value,) + others)


def spread(copies):
    return lax.all_to_all(copies, "z", 0, 0)


def pad_rows(parts, rows):
    have = sum(p.shape[0] for p in parts)
    if have < rows:
        parts = parts + [jnp.zeros((rows - have, LANES), parts[0].dtype)]
    return jnp.concatenate(parts, axis=0)


def nn(a, b):
    return jnp.dot(a, b, preferred_element_type=f32)


def nt(a, b):
    return lax.dot_general(a, b, (((1,), (1,)), ((), ())), preferred_element_type=f32)


def target_of(q, core, yl, z, rank, up_rows):
    j = q % EXTRA
    block = q // EXTRA
    of_core = jnp.where(block // (2 * z) == 0, core, 1 - core)
    of_yl = jnp.where((block // z) % 2 == 0, yl, 1 - yl)
    row = (block % z) * 4 + of_yl * 2 + of_core
    return jnp.where(j < up_rows, j * rank + row, jnp.where(j < up_rows + 2, up_rows * rank + j - up_rows, -1))


def unpack(core, yl, quarters, down, extra, rank):
    z = quarters[0].shape[0]
    for quarter, ref in enumerate(quarters):
        of_core = core if quarter < 2 else 1 - core
        of_yl = yl if quarter % 2 == 0 else 1 - yl
        offset = (of_yl * 2 + of_core) * LANES
        for i in range(z):
            at = pl.multiple_of(i * 4 * LANES + offset, LANES)
            down[:, pl.ds(at, LANES)] = ref[i, :rank, :]
            row = (quarter * z + i) * EXTRA
            extra[row : row + EXTRA, :] = ref[i, rank:, :]


def up_rows_of(core, yl, extra, z, rank, up_rows):
    places = up_rows * rank + 16
    shape = (places, extra.shape[0])
    q = lax.broadcasted_iota(jnp.int32, (1, shape[1]), 1)
    pick = lax.broadcasted_iota(jnp.int32, shape, 0) == target_of(q, core, yl, z, rank, up_rows)
    found = nn(pick.astype(f32).astype(bf16), extra[...])
    up = jnp.concatenate(
        [found[k * rank : (k + 1) * rank].astype(bf16) for k in range(up_rows)], axis=1
    )
    return up, found[up_rows * rank :]


def prepare_kernel(down_master, up_master, loss_weight, value_weight, copies, weights):
    rank = down_master.shape[0]
    features = up_master.shape[1]
    down = down_master[...].astype(bf16)
    count = jnp.sum(loss_weight[...].astype(f32), axis=1, keepdims=True)
    high = jnp.floor(count / 128.0)
    parts = [up_master[:, at : at + LANES] for at in range(0, features, LANES)]
    parts += [jnp.broadcast_to(c, (1, LANES)) for c in (high, count - 128.0 * high)]
    parts.append(jnp.zeros((EXTRA - len(parts), LANES), f32))
    extra = jnp.concatenate(parts, axis=0).astype(bf16)
    for i in range(copies.shape[0]):
        copies[i, :rank, :] = down
        copies[i, rank:, :] = extra
    weights[:features, :] = value_weight[...].astype(f32).T.astype(bf16)
    weights[features:, :] = down


def backward_kernel(
    place, q0, q1, q2, q3, acts, value_grad, loss_weight, keep, send, rows_out, down, extra
):
    core, yl = place[0], place[1]
    z = q0.shape[0]
    rank = down.shape[0]
    tokens, features = value_grad.shape
    up_rows = features // LANES
    unpack(core, yl, (q0, q1, q2, q3), down, extra, rank)
    up, counts = up_rows_of(core, yl, extra, z, rank, up_rows)
    total = counts[0:1, :1] * 128.0 + counts[1:2, :1]
    weight = jnp.broadcast_to(loss_weight[...].astype(f32), (tokens, tokens))
    square = (tokens, tokens)
    diagonal = lax.broadcasted_iota(jnp.int32, square, 0) == lax.broadcasted_iota(jnp.int32, square, 1)
    share = jnp.sum(jnp.where(diagonal, weight, 0.0), axis=1, keepdims=True) / total
    scaled = (value_grad[...].astype(f32) * share).astype(bf16)
    rows_out[:, :features] = scaled
    rows_out[:, features:] = (adapter_scale * nt(scaled, up)).astype(bf16)
    mid_t = (adapter_scale * nt(up, scaled)).astype(bf16)
    low_t = nt(down[...], acts[...]).astype(bf16)

    shape = (extra.shape[0], up_rows * rank)
    q = lax.broadcasted_iota(jnp.int32, (shape[0], 1), 0)
    put = lax.broadcasted_iota(jnp.int32, shape, 1) == target_of(q, core, yl, z, rank, up_rows)
    put = put.astype(f32).astype(bf16)
    up_grad = jnp.zeros((shape[0], LANES), f32)
    for k in range(up_rows):
        low_k = nn(put[:, k * rank : (k + 1) * rank], low_t).astype(bf16)
        up_grad = up_grad + nn(low_k, scaled[:, k * LANES : (k + 1) * LANES])
    up_grad = adapter_scale * up_grad

    for half in range(2):
        of_yl = yl if half == 0 else 1 - yl
        for i in range(z):
            at = pl.multiple_of(i * 4 * LANES + of_yl * 2 * LANES, 2 * LANES)
            grad = nn(mid_t, acts[:, pl.ds(at, 2 * LANES)])
            first, second = grad[:, :LANES], grad[:, LANES:]
            row = (half * z + i) * EXTRA
            keep[half, i, :rank, :] = jnp.where(core == 0, first, second)
            keep[half, i, rank:, :] = up_grad[row : row + EXTRA]
            row = ((2 + half) * z + i) * EXTRA
            send[half, i, :rank, :] = jnp.where(core == 0, second, first).astype(bf16)
            send[half, i, rank:, :] = up_grad[row : row + EXTRA].astype(bf16)


def refresh_kernel(place, q0, q1, q2, q3, acts, out, down, extra):
    core, yl = place[0], place[1]
    rank = down.shape[0]
    unpack(core, yl, (q0, q1, q2, q3), down, extra, rank)
    up, _ = up_rows_of(core, yl, extra, q0.shape[0], rank, out.shape[1] // LANES)
    low = nt(acts[...], down[...]).astype(bf16)
    out[...] = (adapter_scale * nn(low, up)).astype(bf16)


def columns_kernel(rows_mine, rows_other, weights, mine, other, held, sems):
    chunks = sems.shape[0]
    size = held.shape[0] // chunks
    parts = [pl.ds(k * size, size) for k in range(chunks)]
    copies = [
        pltpu.make_async_copy(weights.at[part], held.at[part], sems.at[k])
        for k, part in enumerate(parts)
    ]
    for copy in copies:
        copy.start()
    for k in range(chunks):
        copies[k].wait()
        for i in range(k * size, (k + 1) * size, 2):
            pair = jnp.concatenate([held[i], held[i + 1]], axis=1)
            mine[:, i * LANES : (i + 2) * LANES] = nn(rows_mine[...], pair).astype(bf16)
            other[:, i * LANES : (i + 2) * LANES] = nn(rows_other[...], pair).astype(bf16)


def merge_kernel(place, mine, other, out):
    core = place[0]
    for i in range(mine.shape[1] // LANES):
        a, b = mine[:, i * LANES : (i + 1) * LANES], other[:, i * LANES : (i + 1) * LANES]
        at = i * 2 * LANES
        out[:, at : at + LANES] = jnp.where(core == 0, a, b)
        out[:, at + LANES : at + 2 * LANES] = jnp.where(core == 0, b, a)


def whole(n):
    return [pl.BlockSpec(memory_space=pltpu.VMEM)] * n


SCALARS = pl.BlockSpec(memory_space=pltpu.SMEM)


def per_device(
    acts,
    value_grad,
    loss_weight,
    value_weight,
    down_master,
    down_first,
    down_second,
    up_master,
    up_first,
    up_second,
    step_count,
):
    tokens, width = acts.shape[1:]
    features = value_grad.shape[2]
    rank = down_master.shape[2]
    up_rows = features // LANES
    rows = rank + EXTRA
    z, sections = lax.axis_size("z"), lax.axis_size("section")
    place = jnp.stack([lax.axis_index("core"), lax.axis_index("yl")]).astype(jnp.int32)
    params = pltpu.CompilerParams(vmem_limit_bytes=VMEM_BYTES)
    acts = acts[0]
    copies, weights = pl.pallas_call(
        prepare_kernel,
        out_shape=(
            jax.ShapeDtypeStruct((z, rows, LANES), bf16),
            jax.ShapeDtypeStruct((features + rank, LANES), bf16),
        ),
        in_specs=whole(4),
        out_specs=tuple(whole(2)),
        compiler_params=pltpu.CompilerParams(vmem_limit_bytes=60 * 1024 * 1024),
        name="prepare",
    )(down_master[0].T, up_master[0], loss_weight, value_weight[0])

    def from_next(flip):
        return [
            (s * 2 + (yl ^ flip), (s - 1) * 2 + yl) for s in range(1, sections) for yl in range(2)
        ]

    same = lax.ppermute(weights, ("section", "yl"), from_next(0))
    flipped = lax.ppermute(weights, ("section", "yl"), from_next(1))

    got = spread(copies)
    even = lax.axis_index("yl") == 0
    weights = jnp.stack([jnp.where(even, same, flipped), jnp.where(even, flipped, same)])
    got_yl, weights = after(swap(got, "yl"), weights)
    weights_all = lax.all_gather(weights, "z").reshape(2 * z, features + rank, LANES)

    keep, send, next_rows = pl.pallas_call(
        backward_kernel,
        out_shape=(
            jax.ShapeDtypeStruct((2, z, rows, LANES), f32),
            jax.ShapeDtypeStruct((2, z, rows, LANES), bf16),
            jax.ShapeDtypeStruct((tokens, features + rank), bf16),
        ),
        in_specs=[SCALARS] + whole(7),
        out_specs=tuple(whole(3)),
        scratch_shapes=[
            pltpu.VMEM((rank, width), bf16),
            pltpu.VMEM((4 * z * EXTRA, LANES), bf16),
        ],
        compiler_params=params,
        name="backward",
    )(place, got, got_yl, swap(got, "core"), swap(got_yl, "core"), acts, value_grad[0], loss_weight)
    rows_mine, rows_other = [
        lax.ppermute(
            next_rows,
            ("section", "core"),
            [(s * 2 + (c ^ flip), (s - 1) * 2 + c) for s in range(1, sections) for c in range(2)],
        )
        for flip in range(2)
    ]

    kept = keep + swap(send, "core").astype(f32)
    kept = kept[0] + swap(kept[1].astype(bf16), "yl").astype(f32)
    parts = lax.all_to_all(kept.astype(bf16), "z", 0, 0)
    parts, rows_mine, rows_other = after(parts, rows_mine, rows_other)
    grad = jnp.sum(parts.astype(f32), axis=0)

    count = step_count.astype(f32)[0]
    down_new, down_first_new, down_second_new = adam_update(
        down_master[0].T, down_first[0].T, down_second[0].T, grad[:rank], count
    )
    up_new, up_first_new, up_second_new = adam_update(
        up_master[0], up_first[0], up_second[0], grad[rank : rank + up_rows].reshape(1, features), count
    )
    block = pad_rows([down_new.astype(bf16), up_new.astype(bf16).reshape(up_rows, LANES)], rows)
    got = spread(jnp.broadcast_to(block[None], (z, rows, LANES)))
    got_yl = swap(got, "yl")
    got_core, got_last = swap(got, "core"), swap(got_yl, "core")
    weights_all, _, _ = after(weights_all, got_last, got_core)
    chunks = 4
    half = jax.ShapeDtypeStruct((tokens, width // 2), bf16)
    mine, other = pl.pallas_call(
        columns_kernel,
        out_shape=(half, half),
        in_specs=whole(2) + [pl.BlockSpec(memory_space=pl.ANY)],
        out_specs=tuple(whole(2)),
        scratch_shapes=[
            pltpu.VMEM((2 * z, features + rank, LANES), bf16),
            pltpu.SemaphoreType.DMA((min(chunks, z),)),
        ],
        compiler_params=pltpu.CompilerParams(vmem_limit_bytes=52 * 1024 * 1024),
        cost_estimate=pl.CostEstimate(
            flops=2 * tokens * (features + rank) * width,
            bytes_accessed=(features + rank) * width,
            transcendentals=0,
        ),
        name="columns",
    )(rows_mine, rows_other, weights_all)
    other = swap(other, "core")
    refreshed = pl.pallas_call(
        refresh_kernel,
        out_shape=jax.ShapeDtypeStruct((tokens, features), bf16),
        in_specs=[SCALARS] + whole(5),
        out_specs=whole(1)[0],
        scratch_shapes=[
            pltpu.VMEM((rank, width), bf16),
            pltpu.VMEM((4 * z * EXTRA, LANES), bf16),
        ],
        compiler_params=params,
        name="refresh",
    )(place, got, got_yl, got_core, got_last, acts)

    other, refreshed = after(other, refreshed)
    steps = 2
    half_spec = pl.BlockSpec((tokens, width // 2 // steps), lambda i: (0, i))
    upstream = pl.pallas_call(
        merge_kernel,
        out_shape=jax.ShapeDtypeStruct((tokens, width), bf16),
        grid=(steps,),
        in_specs=[SCALARS, half_spec, half_spec],
        out_specs=pl.BlockSpec((tokens, width // steps), lambda i: (0, i)),
        compiler_params=params,
        name="merge",
    )(place, mine, other)
    return (
        upstream[None],
        refreshed[None],
        down_new.T[None],
        down_first_new.T[None],
        down_second_new.T[None],
        up_new[None],
        up_first_new[None],
        up_second_new[None],
    )


def solution(mesh):
    sections, dp = mesh.devices.shape
    staged = Mesh(mesh.devices.reshape(sections, dp // 4, 2, 2), ("section", "z", "yl", "core"))
    split = P("section", ("z", "yl", "core"))
    return jax.shard_map(
        per_device,
        mesh=staged,
        in_specs=(split,) * 10 + (P(),),
        out_specs=(split,) * 8,
        check_vma=False,
    )
```

```python
import jax
import jax.numpy as jnp
from jax import lax
from jax.experimental import pallas as pl
from jax.experimental.pallas import tpu as pltpu
from jax.sharding import Mesh, PartitionSpec as P

adapter_scale = 2.0
beta_one = 0.9
beta_two = 0.999
learn_rate = 0.05
adam_eps = 1e-08

LANES = 128
EXTRA = 8
bf16 = jnp.bfloat16
f32 = jnp.float32
VMEM_BYTES = 20 * 1024 * 1024


def adam_update(master, first, second, grad, count):
    first_new = beta_one * first + (1.0 - beta_one) * grad
    second_new = beta_two * second + (1.0 - beta_two) * grad * grad
    fix_first = 1.0 - jnp.power(jnp.float32(beta_one), count)
    fix_second = 1.0 - jnp.power(jnp.float32(beta_two), count)
    master_new = master - learn_rate * (first_new / fix_first) / (
        jnp.sqrt(second_new / fix_second) + adam_eps
    )
    return (master_new, first_new, second_new)


def swap(array, axis):
    return lax.ppermute(array, axis, [(0, 1), (1, 0)])


def after(value, *others):
    return lax.optimization_barrier((value,) + others)


def spread(copies):
    return lax.all_to_all(copies, "z", 0, 0)


def pad_rows(parts, rows):
    have = sum(p.shape[0] for p in parts)
    if have < rows:
        parts = parts + [jnp.zeros((rows - have, LANES), parts[0].dtype)]
    return jnp.concatenate(parts, axis=0)


def nn(a, b):
    return jnp.dot(a, b, preferred_element_type=f32)


def nt(a, b):
    return lax.dot_general(a, b, (((1,), (1,)), ((), ())), preferred_element_type=f32)


def target_of(q, core, yl, z, rank, up_rows):
    j = q % EXTRA
    block = q // EXTRA
    of_core = jnp.where(block // (2 * z) == 0, core, 1 - core)
    of_yl = jnp.where((block // z) % 2 == 0, yl, 1 - yl)
    row = (block % z) * 4 + of_yl * 2 + of_core
    return jnp.where(j < up_rows, j * rank + row, jnp.where(j < up_rows + 2, up_rows * rank + j - up_rows, -1))


def unpack(core, yl, quarters, down, extra, rank):
    z = quarters[0].shape[0]
    for quarter, ref in enumerate(quarters):
        of_core = core if quarter < 2 else 1 - core
        of_yl = yl if quarter % 2 == 0 else 1 - yl
        offset = (of_yl * 2 + of_core) * LANES
        for i in range(z):
            at = pl.multiple_of(i * 4 * LANES + offset, LANES)
            down[:, pl.ds(at, LANES)] = ref[i, :rank, :]
            row = (quarter * z + i) * EXTRA
            extra[row : row + EXTRA, :] = ref[i, rank:, :]


def up_rows_of(core, yl, extra, z, rank, up_rows):
    places = up_rows * rank + 16
    shape = (places, extra.shape[0])
    q = lax.broadcasted_iota(jnp.int32, (1, shape[1]), 1)
    pick = lax.broadcasted_iota(jnp.int32, shape, 0) == target_of(q, core, yl, z, rank, up_rows)
    found = nn(pick.astype(f32).astype(bf16), extra[...])
    up = jnp.concatenate(
        [found[k * rank : (k + 1) * rank].astype(bf16) for k in range(up_rows)], axis=1
    )
    return up, found[up_rows * rank :]


def prepare_kernel(down_master, up_master, loss_weight, value_weight, copies, weights):
    rank = down_master.shape[0]
    features = up_master.shape[1]
    down = down_master[...].astype(bf16)
    count = jnp.sum(loss_weight[...].astype(f32), axis=1, keepdims=True)
    high = jnp.floor(count / 128.0)
    parts = [up_master[:, at : at + LANES] for at in range(0, features, LANES)]
    parts += [jnp.broadcast_to(c, (1, LANES)) for c in (high, count - 128.0 * high)]
    parts.append(jnp.zeros((EXTRA - len(parts), LANES), f32))
    extra = jnp.concatenate(parts, axis=0).astype(bf16)
    for i in range(copies.shape[0]):
        copies[i, :rank, :] = down
        copies[i, rank:, :] = extra
    weights[:features, :] = value_weight[...].astype(f32).T.astype(bf16)
    weights[features:, :] = down


def backward_kernel(
    place, q0, q1, q2, q3, acts, value_grad, loss_weight, keep, send, rows_out, down, extra
):
    core, yl = place[0], place[1]
    z = q0.shape[0]
    rank = down.shape[0]
    tokens, features = value_grad.shape
    up_rows = features // LANES
    unpack(core, yl, (q0, q1, q2, q3), down, extra, rank)
    up, counts = up_rows_of(core, yl, extra, z, rank, up_rows)
    total = counts[0:1, :1] * 128.0 + counts[1:2, :1]
    weight = jnp.broadcast_to(loss_weight[...].astype(f32), (tokens, tokens))
    square = (tokens, tokens)
    diagonal = lax.broadcasted_iota(jnp.int32, square, 0) == lax.broadcasted_iota(jnp.int32, square, 1)
    share = jnp.sum(jnp.where(diagonal, weight, 0.0), axis=1, keepdims=True) / total
    scaled = (value_grad[...].astype(f32) * share).astype(bf16)
    rows_out[:tokens, :features] = scaled
    rows_out[:tokens, features:] = (adapter_scale * nt(scaled, up)).astype(bf16)
    if rows_out.shape[0] > tokens:
        rows_out[tokens:, :] = jnp.zeros((rows_out.shape[0] - tokens, rows_out.shape[1]), bf16)
    mid_t = (adapter_scale * nt(up, scaled)).astype(bf16)
    low_t = nt(down[...], acts[...]).astype(bf16)

    shape = (extra.shape[0], up_rows * rank)
    q = lax.broadcasted_iota(jnp.int32, (shape[0], 1), 0)
    put = lax.broadcasted_iota(jnp.int32, shape, 1) == target_of(q, core, yl, z, rank, up_rows)
    put = put.astype(f32).astype(bf16)
    up_grad = jnp.zeros((shape[0], LANES), f32)
    for k in range(up_rows):
        low_k = nn(put[:, k * rank : (k + 1) * rank], low_t).astype(bf16)
        up_grad = up_grad + nn(low_k, scaled[:, k * LANES : (k + 1) * LANES])
    up_grad = adapter_scale * up_grad

    for half in range(2):
        of_yl = yl if half == 0 else 1 - yl
        for i in range(z):
            at = pl.multiple_of(i * 4 * LANES + of_yl * 2 * LANES, 2 * LANES)
            grad = nn(mid_t, acts[:, pl.ds(at, 2 * LANES)])
            first, second = grad[:, :LANES], grad[:, LANES:]
            row = (half * z + i) * EXTRA
            keep[half, i, :rank, :] = jnp.where(core == 0, first, second)
            keep[half, i, rank:, :] = up_grad[row : row + EXTRA]
            row = ((2 + half) * z + i) * EXTRA
            send[half, i, :rank, :] = jnp.where(core == 0, second, first).astype(bf16)
            send[half, i, rank:, :] = up_grad[row : row + EXTRA].astype(bf16)


def refresh_kernel(place, q0, q1, q2, q3, acts, out, down, extra):
    core, yl = place[0], place[1]
    rank = down.shape[0]
    unpack(core, yl, (q0, q1, q2, q3), down, extra, rank)
    up, _ = up_rows_of(core, yl, extra, q0.shape[0], rank, out.shape[1] // LANES)
    low = nt(acts[...], down[...]).astype(bf16)
    out[...] = (adapter_scale * nn(low, up)).astype(bf16)


def columns_kernel(rows_mine, rows_other, weights, mine, other, rows, held, sems):
    tokens, second = mine.shape[0], rows_mine.shape[0]
    chunks = sems.shape[0] - 2
    size = held.shape[0] // chunks
    copies = [
        pltpu.make_async_copy(rows_mine, rows.at[pl.ds(0, second)], sems.at[chunks]),
        pltpu.make_async_copy(rows_other, rows.at[pl.ds(second, second)], sems.at[chunks + 1]),
    ]
    for k in range(chunks):
        part = pl.ds(k * size, size)
        copies.append(pltpu.make_async_copy(weights.at[part], held.at[part], sems.at[k]))
    for copy in copies:
        copy.start()
    copies[0].wait()
    copies[1].wait()
    for k in range(chunks):
        copies[k + 2].wait()
        for i in range(k * size, (k + 1) * size, 2):
            product = nn(rows[...], jnp.concatenate([held[i], held[i + 1]], axis=1))
            mine[:, i * LANES : (i + 2) * LANES] = product[:tokens].astype(bf16)
            other[:, i * LANES : (i + 2) * LANES] = product[second : second + tokens].astype(bf16)


def merge_kernel(place, mine, other, out):
    core = place[0]
    for i in range(mine.shape[1] // LANES):
        a, b = mine[:, i * LANES : (i + 1) * LANES], other[:, i * LANES : (i + 1) * LANES]
        at = i * 2 * LANES
        out[:, at : at + LANES] = jnp.where(core == 0, a, b)
        out[:, at + LANES : at + 2 * LANES] = jnp.where(core == 0, b, a)


def whole(n):
    return [pl.BlockSpec(memory_space=pltpu.VMEM)] * n


SCALARS = pl.BlockSpec(memory_space=pltpu.SMEM)


def per_device(
    acts,
    value_grad,
    loss_weight,
    value_weight,
    down_master,
    down_first,
    down_second,
    up_master,
    up_first,
    up_second,
    step_count,
):
    tokens, width = acts.shape[1:]
    features = value_grad.shape[2]
    rank = down_master.shape[2]
    up_rows = features // LANES
    rows = rank + EXTRA
    padded = -(-tokens // 16) * 16
    z, sections = lax.axis_size("z"), lax.axis_size("section")
    place = jnp.stack([lax.axis_index("core"), lax.axis_index("yl")]).astype(jnp.int32)
    params = pltpu.CompilerParams(vmem_limit_bytes=VMEM_BYTES)
    acts = acts[0]
    copies, weights = pl.pallas_call(
        prepare_kernel,
        out_shape=(
            jax.ShapeDtypeStruct((z, rows, LANES), bf16),
            jax.ShapeDtypeStruct((features + rank, LANES), bf16),
        ),
        in_specs=whole(4),
        out_specs=tuple(whole(2)),
        compiler_params=pltpu.CompilerParams(vmem_limit_bytes=60 * 1024 * 1024),
        name="prepare",
    )(down_master[0].T, up_master[0], loss_weight, value_weight[0])

    def from_next(flip):
        return [
            (s * 2 + (yl ^ flip), (s - 1) * 2 + yl) for s in range(1, sections) for yl in range(2)
        ]

    same = lax.ppermute(weights, ("section", "yl"), from_next(0))
    flipped = lax.ppermute(weights, ("section", "yl"), from_next(1))

    got = spread(copies)
    even = lax.axis_index("yl") == 0
    weights = jnp.stack([jnp.where(even, same, flipped), jnp.where(even, flipped, same)])
    got, weights = after(got, weights)
    got_yl = swap(got, "yl")
    weights_all = lax.all_gather(weights, "z").reshape(2 * z, features + rank, LANES)

    keep, send, next_rows = pl.pallas_call(
        backward_kernel,
        out_shape=(
            jax.ShapeDtypeStruct((2, z, rows, LANES), f32),
            jax.ShapeDtypeStruct((2, z, rows, LANES), bf16),
            jax.ShapeDtypeStruct((padded, features + rank), bf16),
        ),
        in_specs=[SCALARS] + whole(7),
        out_specs=tuple(whole(3)),
        scratch_shapes=[
            pltpu.VMEM((rank, width), bf16),
            pltpu.VMEM((4 * z * EXTRA, LANES), bf16),
        ],
        compiler_params=params,
        name="backward",
    )(place, got, got_yl, swap(got, "core"), swap(got_yl, "core"), acts, value_grad[0], loss_weight)
    rows_mine, rows_other = [
        lax.ppermute(
            next_rows,
            ("section", "core"),
            [(s * 2 + (c ^ flip), (s - 1) * 2 + c) for s in range(1, sections) for c in range(2)],
        )
        for flip in range(2)
    ]

    kept = keep + swap(send, "core").astype(f32)
    kept = kept[0] + swap(kept[1].astype(bf16), "yl").astype(f32)
    parts = lax.all_to_all(kept.astype(bf16), "z", 0, 0)
    parts, rows_mine, rows_other = after(parts, rows_mine, rows_other)
    grad = jnp.sum(parts.astype(f32), axis=0)

    count = step_count.astype(f32)[0]
    down_new, down_first_new, down_second_new = adam_update(
        down_master[0].T, down_first[0].T, down_second[0].T, grad[:rank], count
    )
    up_new, up_first_new, up_second_new = adam_update(
        up_master[0], up_first[0], up_second[0], grad[rank : rank + up_rows].reshape(1, features), count
    )
    block = pad_rows([down_new.astype(bf16), up_new.astype(bf16).reshape(up_rows, LANES)], rows)
    got = spread(jnp.broadcast_to(block[None], (z, rows, LANES)))
    weights_all, _ = after(weights_all, got)
    chunks = min(4, z)
    half = jax.ShapeDtypeStruct((tokens, width // 2), bf16)
    mine, other = pl.pallas_call(
        columns_kernel,
        out_shape=(half, half),
        in_specs=[pl.BlockSpec(memory_space=pl.ANY)] * 3,
        out_specs=tuple(whole(2)),
        scratch_shapes=[
            pltpu.VMEM((2 * padded, features + rank), bf16),
            pltpu.VMEM((2 * z, features + rank, LANES), bf16),
            pltpu.SemaphoreType.DMA((chunks + 2,)),
        ],
        compiler_params=pltpu.CompilerParams(vmem_limit_bytes=52 * 1024 * 1024),
        cost_estimate=pl.CostEstimate(
            flops=2 * tokens * (features + rank) * width,
            bytes_accessed=(features + rank) * width,
            transcendentals=0,
        ),
        name="columns",
    )(rows_mine, rows_other, weights_all)
    got_yl, mine, other = after(swap(got, "yl"), mine, other)
    got_last, got_core, other = swap(got_yl, "core"), swap(got, "core"), swap(other, "core")
    refreshed = pl.pallas_call(
        refresh_kernel,
        out_shape=jax.ShapeDtypeStruct((tokens, features), bf16),
        in_specs=[SCALARS] + whole(5),
        out_specs=whole(1)[0],
        scratch_shapes=[
            pltpu.VMEM((rank, width), bf16),
            pltpu.VMEM((4 * z * EXTRA, LANES), bf16),
        ],
        compiler_params=params,
        name="refresh",
    )(place, got, got_yl, got_core, got_last, acts)

    other, refreshed = after(other, refreshed)
    steps = 2
    half_spec = pl.BlockSpec((tokens, width // 2 // steps), lambda i: (0, i))
    upstream = pl.pallas_call(
        merge_kernel,
        out_shape=jax.ShapeDtypeStruct((tokens, width), bf16),
        grid=(steps,),
        in_specs=[SCALARS, half_spec, half_spec],
        out_specs=pl.BlockSpec((tokens, width // steps), lambda i: (0, i)),
        compiler_params=params,
        name="merge",
    )(place, mine, other)
    return (
        upstream[None],
        refreshed[None],
        down_new.T[None],
        down_first_new.T[None],
        down_second_new.T[None],
        up_new[None],
        up_first_new[None],
        up_second_new[None],
    )


def solution(mesh):
    sections, dp = mesh.devices.shape
    staged = Mesh(mesh.devices.reshape(sections, dp // 4, 2, 2), ("section", "z", "yl", "core"))
    split = P("section", ("z", "yl", "core"))
    return jax.shard_map(
        per_device,
        mesh=staged,
        in_specs=(split,) * 10 + (P(),),
        out_specs=(split,) * 8,
        check_vma=False,
    )
```

```python
import jax
import jax.numpy as jnp
from jax import lax
from jax.experimental import pallas as pl
from jax.experimental.pallas import tpu as pltpu
from jax.sharding import Mesh, PartitionSpec as P

adapter_scale = 2.0
beta_one = 0.9
beta_two = 0.999
learn_rate = 0.05
adam_eps = 1e-08

LANES = 128
EXTRA = 8
bf16 = jnp.bfloat16
f32 = jnp.float32
VMEM_BYTES = 20 * 1024 * 1024


def adam_update(master, first, second, grad, count):
    first_new = beta_one * first + (1.0 - beta_one) * grad
    second_new = beta_two * second + (1.0 - beta_two) * grad * grad
    fix_first = 1.0 - jnp.power(jnp.float32(beta_one), count)
    fix_second = 1.0 - jnp.power(jnp.float32(beta_two), count)
    master_new = master - learn_rate * (first_new / fix_first) / (
        jnp.sqrt(second_new / fix_second) + adam_eps
    )
    return (master_new, first_new, second_new)


def swap(array, axis):
    return lax.ppermute(array, axis, [(0, 1), (1, 0)])


def after(value, *others):
    return lax.optimization_barrier((value,) + others)


def spread(copies):
    return lax.all_to_all(copies, "z", 0, 0)


def pad_rows(parts, rows):
    have = sum(p.shape[0] for p in parts)
    if have < rows:
        parts = parts + [jnp.zeros((rows - have, LANES), parts[0].dtype)]
    return jnp.concatenate(parts, axis=0)


def nn(a, b):
    return jnp.dot(a, b, preferred_element_type=f32)


def nt(a, b):
    return lax.dot_general(a, b, (((1,), (1,)), ((), ())), preferred_element_type=f32)


def target_of(q, core, yl, z, rank, up_rows):
    j = q % EXTRA
    block = q // EXTRA
    of_core = jnp.where(block // (2 * z) == 0, core, 1 - core)
    of_yl = jnp.where((block // z) % 2 == 0, yl, 1 - yl)
    row = (block % z) * 4 + of_yl * 2 + of_core
    return jnp.where(j < up_rows, j * rank + row, jnp.where(j < up_rows + 2, up_rows * rank + j - up_rows, -1))


def unpack(core, yl, quarters, down, extra, rank):
    z = quarters[0].shape[0]
    for quarter, ref in enumerate(quarters):
        of_core = core if quarter < 2 else 1 - core
        of_yl = yl if quarter % 2 == 0 else 1 - yl
        offset = (of_yl * 2 + of_core) * LANES
        for i in range(z):
            at = pl.multiple_of(i * 4 * LANES + offset, LANES)
            down[:, pl.ds(at, LANES)] = ref[i, :rank, :]
            row = (quarter * z + i) * EXTRA
            extra[row : row + EXTRA, :] = ref[i, rank:, :]


def up_rows_of(core, yl, extra, z, rank, up_rows):
    places = up_rows * rank + 16
    shape = (places, extra.shape[0])
    q = lax.broadcasted_iota(jnp.int32, (1, shape[1]), 1)
    pick = lax.broadcasted_iota(jnp.int32, shape, 0) == target_of(q, core, yl, z, rank, up_rows)
    found = nn(pick.astype(f32).astype(bf16), extra[...])
    up = jnp.concatenate(
        [found[k * rank : (k + 1) * rank].astype(bf16) for k in range(up_rows)], axis=1
    )
    return up, found[up_rows * rank :]


def prepare_kernel(down_master, up_master, loss_weight, value_weight, copies, weights):
    rank = down_master.shape[0]
    features = up_master.shape[1]
    down = down_master[...].astype(bf16)
    count = jnp.sum(loss_weight[...].astype(f32), axis=1, keepdims=True)
    high = jnp.floor(count / 128.0)
    parts = [up_master[:, at : at + LANES] for at in range(0, features, LANES)]
    parts += [jnp.broadcast_to(c, (1, LANES)) for c in (high, count - 128.0 * high)]
    parts.append(jnp.zeros((EXTRA - len(parts), LANES), f32))
    extra = jnp.concatenate(parts, axis=0).astype(bf16)
    for i in range(copies.shape[0]):
        copies[i, :rank, :] = down
        copies[i, rank:, :] = extra
    weights[:features, :] = value_weight[...].astype(f32).T.astype(bf16)
    weights[features:, :] = down


def backward_kernel(
    place, q0, q1, q2, q3, acts, value_grad, loss_weight, keep, send, rows_out, down, extra
):
    core, yl = place[0], place[1]
    z = q0.shape[0]
    rank = down.shape[0]
    tokens, features = value_grad.shape
    up_rows = features // LANES
    unpack(core, yl, (q0, q1, q2, q3), down, extra, rank)
    up, counts = up_rows_of(core, yl, extra, z, rank, up_rows)
    total = counts[0:1, :1] * 128.0 + counts[1:2, :1]
    weight = jnp.broadcast_to(loss_weight[...].astype(f32), (tokens, tokens))
    square = (tokens, tokens)
    diagonal = lax.broadcasted_iota(jnp.int32, square, 0) == lax.broadcasted_iota(jnp.int32, square, 1)
    share = jnp.sum(jnp.where(diagonal, weight, 0.0), axis=1, keepdims=True) / total
    scaled = (value_grad[...].astype(f32) * share).astype(bf16)
    rows_out[:tokens, :features] = scaled
    rows_out[:tokens, features:] = (adapter_scale * nt(scaled, up)).astype(bf16)
    if rows_out.shape[0] > tokens:
        rows_out[tokens:, :] = jnp.zeros((rows_out.shape[0] - tokens, rows_out.shape[1]), bf16)
    mid_t = (adapter_scale * nt(up, scaled)).astype(bf16)
    low_t = nt(down[...], acts[...]).astype(bf16)

    shape = (extra.shape[0], up_rows * rank)
    q = lax.broadcasted_iota(jnp.int32, (shape[0], 1), 0)
    put = lax.broadcasted_iota(jnp.int32, shape, 1) == target_of(q, core, yl, z, rank, up_rows)
    put = put.astype(f32).astype(bf16)
    up_grad = jnp.zeros((shape[0], LANES), f32)
    for k in range(up_rows):
        low_k = nn(put[:, k * rank : (k + 1) * rank], low_t).astype(bf16)
        up_grad = up_grad + nn(low_k, scaled[:, k * LANES : (k + 1) * LANES])
    up_grad = adapter_scale * up_grad

    for half in range(2):
        of_yl = yl if half == 0 else 1 - yl
        for i in range(z):
            at = pl.multiple_of(i * 4 * LANES + of_yl * 2 * LANES, 2 * LANES)
            grad = nn(mid_t, acts[:, pl.ds(at, 2 * LANES)])
            first, second = grad[:, :LANES], grad[:, LANES:]
            row = (half * z + i) * EXTRA
            keep[half, i, :rank, :] = jnp.where(core == 0, first, second)
            keep[half, i, rank:, :] = up_grad[row : row + EXTRA]
            row = ((2 + half) * z + i) * EXTRA
            send[half, i, :rank, :] = jnp.where(core == 0, second, first).astype(bf16)
            send[half, i, rank:, :] = up_grad[row : row + EXTRA].astype(bf16)


def refresh_kernel(place, q0, q1, q2, q3, acts, out, down, extra):
    core, yl = place[0], place[1]
    rank = down.shape[0]
    unpack(core, yl, (q0, q1, q2, q3), down, extra, rank)
    up, _ = up_rows_of(core, yl, extra, q0.shape[0], rank, out.shape[1] // LANES)
    low = nt(acts[...], down[...]).astype(bf16)
    out[...] = (adapter_scale * nn(low, up)).astype(bf16)


def columns_kernel(rows_mine, rows_other, weights, mine, other, rows, held, sems):
    tokens, second = mine.shape[0], rows_mine.shape[0]
    chunks = sems.shape[0] - 2
    size = held.shape[0] // chunks
    copies = [
        pltpu.make_async_copy(rows_mine, rows.at[pl.ds(0, second)], sems.at[chunks]),
        pltpu.make_async_copy(rows_other, rows.at[pl.ds(second, second)], sems.at[chunks + 1]),
    ]
    for k in range(chunks):
        part = pl.ds(k * size, size)
        copies.append(pltpu.make_async_copy(weights.at[part], held.at[part], sems.at[k]))
    for copy in copies[:4]:
        copy.start()
    copies[0].wait()
    copies[1].wait()
    for k in range(chunks):
        copies[k + 2].wait()
        if k + 2 < chunks:
            copies[k + 4].start()
        for i in range(k * size, (k + 1) * size, 2):
            product = nn(rows[...], jnp.concatenate([held[i], held[i + 1]], axis=1))
            mine[:, i * LANES : (i + 2) * LANES] = product[:tokens].astype(bf16)
            other[:, i * LANES : (i + 2) * LANES] = product[second : second + tokens].astype(bf16)


def merge_kernel(place, mine, other, out):
    core = place[0]
    for i in range(mine.shape[1] // LANES):
        a, b = mine[:, i * LANES : (i + 1) * LANES], other[:, i * LANES : (i + 1) * LANES]
        at = i * 2 * LANES
        out[:, at : at + LANES] = jnp.where(core == 0, a, b)
        out[:, at + LANES : at + 2 * LANES] = jnp.where(core == 0, b, a)


def whole(n):
    return [pl.BlockSpec(memory_space=pltpu.VMEM)] * n


SCALARS = pl.BlockSpec(memory_space=pltpu.SMEM)


def per_device(
    acts,
    value_grad,
    loss_weight,
    value_weight,
    down_master,
    down_first,
    down_second,
    up_master,
    up_first,
    up_second,
    step_count,
):
    tokens, width = acts.shape[1:]
    features = value_grad.shape[2]
    rank = down_master.shape[2]
    up_rows = features // LANES
    rows = rank + EXTRA
    padded = -(-tokens // 16) * 16
    z, sections = lax.axis_size("z"), lax.axis_size("section")
    place = jnp.stack([lax.axis_index("core"), lax.axis_index("yl")]).astype(jnp.int32)
    params = pltpu.CompilerParams(vmem_limit_bytes=VMEM_BYTES)
    acts = acts[0]
    copies, weights = pl.pallas_call(
        prepare_kernel,
        out_shape=(
            jax.ShapeDtypeStruct((z, rows, LANES), bf16),
            jax.ShapeDtypeStruct((features + rank, LANES), bf16),
        ),
        in_specs=whole(4),
        out_specs=tuple(whole(2)),
        compiler_params=pltpu.CompilerParams(vmem_limit_bytes=60 * 1024 * 1024),
        name="prepare",
    )(down_master[0].T, up_master[0], loss_weight, value_weight[0])

    def from_next(flip):
        return [
            (s * 2 + (yl ^ flip), (s - 1) * 2 + yl) for s in range(1, sections) for yl in range(2)
        ]

    same = lax.ppermute(weights, ("section", "yl"), from_next(0))
    flipped = lax.ppermute(weights, ("section", "yl"), from_next(1))

    got = spread(copies)
    even = lax.axis_index("yl") == 0
    weights = jnp.stack([jnp.where(even, same, flipped), jnp.where(even, flipped, same)])
    got, weights = after(got, weights)
    got_yl = swap(got, "yl")
    weights_all = lax.all_gather(weights, "z").reshape(2 * z, features + rank, LANES)

    keep, send, next_rows = pl.pallas_call(
        backward_kernel,
        out_shape=(
            jax.ShapeDtypeStruct((2, z, rows, LANES), f32),
            jax.ShapeDtypeStruct((2, z, rows, LANES), bf16),
            jax.ShapeDtypeStruct((padded, features + rank), bf16),
        ),
        in_specs=[SCALARS] + whole(7),
        out_specs=tuple(whole(3)),
        scratch_shapes=[
            pltpu.VMEM((rank, width), bf16),
            pltpu.VMEM((4 * z * EXTRA, LANES), bf16),
        ],
        compiler_params=params,
        name="backward",
    )(place, got, got_yl, swap(got, "core"), swap(got_yl, "core"), acts, value_grad[0], loss_weight)
    rows_mine, rows_other = [
        lax.ppermute(
            next_rows,
            ("section", "core"),
            [(s * 2 + (c ^ flip), (s - 1) * 2 + c) for s in range(1, sections) for c in range(2)],
        )
        for flip in range(2)
    ]

    kept = keep + swap(send, "core").astype(f32)
    kept = kept[0] + swap(kept[1].astype(bf16), "yl").astype(f32)
    parts = lax.all_to_all(kept.astype(bf16), "z", 0, 0)
    parts, rows_mine, rows_other = after(parts, rows_mine, rows_other)
    grad = jnp.sum(parts.astype(f32), axis=0)

    count = step_count.astype(f32)[0]
    down_new, down_first_new, down_second_new = adam_update(
        down_master[0].T, down_first[0].T, down_second[0].T, grad[:rank], count
    )
    up_new, up_first_new, up_second_new = adam_update(
        up_master[0], up_first[0], up_second[0], grad[rank : rank + up_rows].reshape(1, features), count
    )
    block = pad_rows([down_new.astype(bf16), up_new.astype(bf16).reshape(up_rows, LANES)], rows)
    got = spread(jnp.broadcast_to(block[None], (z, rows, LANES)))
    got_core = swap(got, "core")
    weights_all, _, _ = after(weights_all, got, got_core)
    chunks = min(4, z)
    half = jax.ShapeDtypeStruct((tokens, width // 2), bf16)
    mine, other = pl.pallas_call(
        columns_kernel,
        out_shape=(half, half),
        in_specs=[pl.BlockSpec(memory_space=pl.ANY)] * 3,
        out_specs=tuple(whole(2)),
        scratch_shapes=[
            pltpu.VMEM((2 * padded, features + rank), bf16),
            pltpu.VMEM((2 * z, features + rank, LANES), bf16),
            pltpu.SemaphoreType.DMA((chunks + 2,)),
        ],
        compiler_params=pltpu.CompilerParams(vmem_limit_bytes=52 * 1024 * 1024),
        cost_estimate=pl.CostEstimate(
            flops=2 * tokens * (features + rank) * width,
            bytes_accessed=(features + rank) * width,
            transcendentals=0,
        ),
        name="columns",
    )(rows_mine, rows_other, weights_all)
    got_yl, mine, other = after(swap(got, "yl"), mine, other)
    got_last = swap(got_yl, "core")
    other, _ = after(other, got_last)
    other = swap(other, "core")
    refreshed = pl.pallas_call(
        refresh_kernel,
        out_shape=jax.ShapeDtypeStruct((tokens, features), bf16),
        in_specs=[SCALARS] + whole(5),
        out_specs=whole(1)[0],
        scratch_shapes=[
            pltpu.VMEM((rank, width), bf16),
            pltpu.VMEM((4 * z * EXTRA, LANES), bf16),
        ],
        compiler_params=params,
        name="refresh",
    )(place, got, got_yl, got_core, got_last, acts)

    other, refreshed = after(other, refreshed)
    steps = 2
    half_spec = pl.BlockSpec((tokens, width // 2 // steps), lambda i: (0, i))
    upstream = pl.pallas_call(
        merge_kernel,
        out_shape=jax.ShapeDtypeStruct((tokens, width), bf16),
        grid=(steps,),
        in_specs=[SCALARS, half_spec, half_spec],
        out_specs=pl.BlockSpec((tokens, width // steps), lambda i: (0, i)),
        compiler_params=params,
        name="merge",
    )(place, mine, other)
    return (
        upstream[None],
        refreshed[None],
        down_new.T[None],
        down_first_new.T[None],
        down_second_new.T[None],
        up_new[None],
        up_first_new[None],
        up_second_new[None],
    )


def solution(mesh):
    sections, dp = mesh.devices.shape
    staged = Mesh(mesh.devices.reshape(sections, dp // 4, 2, 2), ("section", "z", "yl", "core"))
    split = P("section", ("z", "yl", "core"))
    return jax.shard_map(
        per_device,
        mesh=staged,
        in_specs=(split,) * 10 + (P(),),
        out_specs=(split,) * 8,
        check_vma=False,
    )
```

```python
import jax
import jax.numpy as jnp
from jax import lax
from jax.experimental import pallas as pl
from jax.experimental.pallas import tpu as pltpu
from jax.sharding import Mesh, PartitionSpec as P

adapter_scale = 2.0
beta_one = 0.9
beta_two = 0.999
learn_rate = 0.05
adam_eps = 1e-08

LANES = 128
EXTRA = 8
bf16 = jnp.bfloat16
f32 = jnp.float32
VMEM_BYTES = 20 * 1024 * 1024


def adam_update(master, first, second, grad, count):
    first_new = beta_one * first + (1.0 - beta_one) * grad
    second_new = beta_two * second + (1.0 - beta_two) * grad * grad
    fix_first = 1.0 - jnp.power(jnp.float32(beta_one), count)
    fix_second = 1.0 - jnp.power(jnp.float32(beta_two), count)
    master_new = master - learn_rate * (first_new / fix_first) / (
        jnp.sqrt(second_new / fix_second) + adam_eps
    )
    return (master_new, first_new, second_new)


def swap(array, axis):
    return lax.ppermute(array, axis, [(0, 1), (1, 0)])


def after(value, *others):
    return lax.optimization_barrier((value,) + others)


def spread(copies):
    return lax.all_to_all(copies, "z", 0, 0)


def pad_rows(parts, rows):
    have = sum(p.shape[0] for p in parts)
    if have < rows:
        parts = parts + [jnp.zeros((rows - have, LANES), parts[0].dtype)]
    return jnp.concatenate(parts, axis=0)


def nn(a, b):
    return jnp.dot(a, b, preferred_element_type=f32)


def nt(a, b):
    return lax.dot_general(a, b, (((1,), (1,)), ((), ())), preferred_element_type=f32)


def target_of(q, core, yl, z, rank, up_rows):
    j = q % EXTRA
    block = q // EXTRA
    of_core = jnp.where(block // (2 * z) == 0, core, 1 - core)
    of_yl = jnp.where((block // z) % 2 == 0, yl, 1 - yl)
    row = (block % z) * 4 + of_yl * 2 + of_core
    return jnp.where(j < up_rows, j * rank + row, jnp.where(j < up_rows + 2, up_rows * rank + j - up_rows, -1))


def unpack(core, yl, quarters, down, extra, rank):
    z = quarters[0].shape[0]
    for quarter, ref in enumerate(quarters):
        of_core = core if quarter < 2 else 1 - core
        of_yl = yl if quarter % 2 == 0 else 1 - yl
        offset = (of_yl * 2 + of_core) * LANES
        for i in range(z):
            at = pl.multiple_of(i * 4 * LANES + offset, LANES)
            down[:, pl.ds(at, LANES)] = ref[i, :rank, :]
            row = (quarter * z + i) * EXTRA
            extra[row : row + EXTRA, :] = ref[i, rank:, :]


def up_rows_of(core, yl, extra, z, rank, up_rows):
    places = up_rows * rank + 16
    shape = (places, extra.shape[0])
    q = lax.broadcasted_iota(jnp.int32, (1, shape[1]), 1)
    pick = lax.broadcasted_iota(jnp.int32, shape, 0) == target_of(q, core, yl, z, rank, up_rows)
    found = nn(pick.astype(f32).astype(bf16), extra[...])
    up = jnp.concatenate(
        [found[k * rank : (k + 1) * rank].astype(bf16) for k in range(up_rows)], axis=1
    )
    return up, found[up_rows * rank :]


def prepare_kernel(down_master, up_master, loss_weight, value_weight, copies, weights):
    rank = down_master.shape[0]
    features = up_master.shape[1]
    down = down_master[...].astype(bf16)
    count = jnp.sum(loss_weight[...].astype(f32), axis=1, keepdims=True)
    high = jnp.floor(count / 128.0)
    parts = [up_master[:, at : at + LANES] for at in range(0, features, LANES)]
    parts += [jnp.broadcast_to(c, (1, LANES)) for c in (high, count - 128.0 * high)]
    parts.append(jnp.zeros((EXTRA - len(parts), LANES), f32))
    extra = jnp.concatenate(parts, axis=0).astype(bf16)
    for i in range(copies.shape[0]):
        copies[i, :rank, :] = down
        copies[i, rank:, :] = extra
    weights[:features, :] = value_weight[...].astype(f32).T.astype(bf16)
    weights[features:, :] = down


def backward_kernel(
    place, q0, q1, q2, q3, acts, value_grad, loss_weight, keep, send, rows_out, down, extra
):
    core, yl = place[0], place[1]
    z = q0.shape[0]
    rank = down.shape[0]
    tokens, features = value_grad.shape
    up_rows = features // LANES
    unpack(core, yl, (q0, q1, q2, q3), down, extra, rank)
    up, counts = up_rows_of(core, yl, extra, z, rank, up_rows)
    total = counts[0:1, :1] * 128.0 + counts[1:2, :1]
    weight = jnp.broadcast_to(loss_weight[...].astype(f32), (tokens, tokens))
    square = (tokens, tokens)
    diagonal = lax.broadcasted_iota(jnp.int32, square, 0) == lax.broadcasted_iota(jnp.int32, square, 1)
    share = jnp.sum(jnp.where(diagonal, weight, 0.0), axis=1, keepdims=True) / total
    scaled = (value_grad[...].astype(f32) * share).astype(bf16)
    rows_out[:tokens, :features] = scaled
    rows_out[:tokens, features:] = (adapter_scale * nt(scaled, up)).astype(bf16)
    if rows_out.shape[0] > tokens:
        rows_out[tokens:, :] = jnp.zeros((rows_out.shape[0] - tokens, rows_out.shape[1]), bf16)
    mid_t = (adapter_scale * nt(up, scaled)).astype(bf16)
    low_t = nt(down[...], acts[...]).astype(bf16)

    shape = (extra.shape[0], up_rows * rank)
    q = lax.broadcasted_iota(jnp.int32, (shape[0], 1), 0)
    put = lax.broadcasted_iota(jnp.int32, shape, 1) == target_of(q, core, yl, z, rank, up_rows)
    put = put.astype(f32).astype(bf16)
    up_grad = jnp.zeros((shape[0], LANES), f32)
    for k in range(up_rows):
        low_k = nn(put[:, k * rank : (k + 1) * rank], low_t).astype(bf16)
        up_grad = up_grad + nn(low_k, scaled[:, k * LANES : (k + 1) * LANES])
    up_grad = adapter_scale * up_grad

    for half in range(2):
        of_yl = yl if half == 0 else 1 - yl
        for i in range(z):
            at = pl.multiple_of(i * 4 * LANES + of_yl * 2 * LANES, 2 * LANES)
            grad = nn(mid_t, acts[:, pl.ds(at, 2 * LANES)])
            first, second = grad[:, :LANES], grad[:, LANES:]
            row = (half * z + i) * EXTRA
            keep[half, i, :rank, :] = jnp.where(core == 0, first, second)
            keep[half, i, rank:, :] = up_grad[row : row + EXTRA]
            row = ((2 + half) * z + i) * EXTRA
            send[half, i, :rank, :] = jnp.where(core == 0, second, first).astype(bf16)
            send[half, i, rank:, :] = up_grad[row : row + EXTRA].astype(bf16)


def columns_kernel(rows_mine, rows_other, weights, mine, other, rows, held, sems):
    tokens, second = mine.shape[0], rows_mine.shape[0]
    chunks = sems.shape[0] - 2
    size = held.shape[0] // chunks
    copies = [
        pltpu.make_async_copy(rows_mine, rows.at[pl.ds(0, second)], sems.at[chunks]),
        pltpu.make_async_copy(rows_other, rows.at[pl.ds(second, second)], sems.at[chunks + 1]),
    ]
    for k in range(chunks):
        part = pl.ds(k * size, size)
        copies.append(pltpu.make_async_copy(weights.at[part], held.at[part], sems.at[k]))
    for copy in copies:
        copy.start()
    copies[0].wait()
    copies[1].wait()
    for k in range(chunks):
        copies[k + 2].wait()
        for i in range(k * size, (k + 1) * size, 2):
            product = nn(rows[...], jnp.concatenate([held[i], held[i + 1]], axis=1))
            mine[:, i * LANES : (i + 2) * LANES] = product[:tokens].astype(bf16)
            other[:, i * LANES : (i + 2) * LANES] = product[second : second + tokens].astype(bf16)


def finish_kernel(place, q0, q1, q2, q3, acts, mine, other, out, upstream, down, extra, merged, sem):
    core, yl = place[0], place[1]
    rank = down.shape[0]
    for i in range(mine.shape[1] // LANES):
        a, b = mine[:, i * LANES : (i + 1) * LANES], other[:, i * LANES : (i + 1) * LANES]
        at = i * 2 * LANES
        merged[:, at : at + LANES] = jnp.where(core == 0, a, b)
        merged[:, at + LANES : at + 2 * LANES] = jnp.where(core == 0, b, a)
    copy = pltpu.make_async_copy(merged, upstream, sem)
    copy.start()
    unpack(core, yl, (q0, q1, q2, q3), down, extra, rank)
    up, _ = up_rows_of(core, yl, extra, q0.shape[0], rank, out.shape[1] // LANES)
    low = nt(acts[...], down[...]).astype(bf16)
    out[...] = (adapter_scale * nn(low, up)).astype(bf16)
    copy.wait()


def whole(n):
    return [pl.BlockSpec(memory_space=pltpu.VMEM)] * n


SCALARS = pl.BlockSpec(memory_space=pltpu.SMEM)


def per_device(
    acts,
    value_grad,
    loss_weight,
    value_weight,
    down_master,
    down_first,
    down_second,
    up_master,
    up_first,
    up_second,
    step_count,
):
    tokens, width = acts.shape[1:]
    features = value_grad.shape[2]
    rank = down_master.shape[2]
    up_rows = features // LANES
    rows = rank + EXTRA
    padded = -(-tokens // 16) * 16
    z, sections = lax.axis_size("z"), lax.axis_size("section")
    place = jnp.stack([lax.axis_index("core"), lax.axis_index("yl")]).astype(jnp.int32)
    params = pltpu.CompilerParams(vmem_limit_bytes=VMEM_BYTES)
    acts = acts[0]
    copies, weights = pl.pallas_call(
        prepare_kernel,
        out_shape=(
            jax.ShapeDtypeStruct((z, rows, LANES), bf16),
            jax.ShapeDtypeStruct((features + rank, LANES), bf16),
        ),
        in_specs=whole(4),
        out_specs=tuple(whole(2)),
        compiler_params=pltpu.CompilerParams(vmem_limit_bytes=60 * 1024 * 1024),
        name="prepare",
    )(down_master[0].T, up_master[0], loss_weight, value_weight[0])

    def from_next(flip):
        return [
            (s * 2 + (yl ^ flip), (s - 1) * 2 + yl) for s in range(1, sections) for yl in range(2)
        ]

    same = lax.ppermute(weights, ("section", "yl"), from_next(0))
    flipped = lax.ppermute(weights, ("section", "yl"), from_next(1))

    got = spread(copies)
    even = lax.axis_index("yl") == 0
    weights = jnp.stack([jnp.where(even, same, flipped), jnp.where(even, flipped, same)])
    got, weights = after(got, weights)
    got_yl = swap(got, "yl")
    weights_all = lax.all_gather(weights, "z").reshape(2 * z, features + rank, LANES)

    keep, send, next_rows = pl.pallas_call(
        backward_kernel,
        out_shape=(
            jax.ShapeDtypeStruct((2, z, rows, LANES), f32),
            jax.ShapeDtypeStruct((2, z, rows, LANES), bf16),
            jax.ShapeDtypeStruct((padded, features + rank), bf16),
        ),
        in_specs=[SCALARS] + whole(7),
        out_specs=tuple(whole(3)),
        scratch_shapes=[
            pltpu.VMEM((rank, width), bf16),
            pltpu.VMEM((4 * z * EXTRA, LANES), bf16),
        ],
        compiler_params=params,
        name="backward",
    )(place, got, got_yl, swap(got, "core"), swap(got_yl, "core"), acts, value_grad[0], loss_weight)
    rows_mine, rows_other = [
        lax.ppermute(
            next_rows,
            ("section", "core"),
            [(s * 2 + (c ^ flip), (s - 1) * 2 + c) for s in range(1, sections) for c in range(2)],
        )
        for flip in range(2)
    ]

    kept = keep + swap(send, "core").astype(f32)
    kept = kept[0] + swap(kept[1].astype(bf16), "yl").astype(f32)
    parts = lax.all_to_all(kept.astype(bf16), "z", 0, 0)
    parts, rows_mine, rows_other = after(parts, rows_mine, rows_other)
    grad = jnp.sum(parts.astype(f32), axis=0)

    count = step_count.astype(f32)[0]
    down_new, down_first_new, down_second_new = adam_update(
        down_master[0].T, down_first[0].T, down_second[0].T, grad[:rank], count
    )
    up_new, up_first_new, up_second_new = adam_update(
        up_master[0], up_first[0], up_second[0], grad[rank : rank + up_rows].reshape(1, features), count
    )
    block = pad_rows([down_new.astype(bf16), up_new.astype(bf16).reshape(up_rows, LANES)], rows)
    got = spread(jnp.broadcast_to(block[None], (z, rows, LANES)))
    weights_all, _ = after(weights_all, got)
    chunks = min(4, z)
    half = jax.ShapeDtypeStruct((tokens, width // 2), bf16)
    mine, other = pl.pallas_call(
        columns_kernel,
        out_shape=(half, half),
        in_specs=[pl.BlockSpec(memory_space=pl.ANY)] * 3,
        out_specs=tuple(whole(2)),
        scratch_shapes=[
            pltpu.VMEM((2 * padded, features + rank), bf16),
            pltpu.VMEM((2 * z, features + rank, LANES), bf16),
            pltpu.SemaphoreType.DMA((chunks + 2,)),
        ],
        compiler_params=pltpu.CompilerParams(vmem_limit_bytes=52 * 1024 * 1024),
        cost_estimate=pl.CostEstimate(
            flops=2 * tokens * (features + rank) * width,
            bytes_accessed=(features + rank) * width,
            transcendentals=0,
        ),
        name="columns",
    )(rows_mine, rows_other, weights_all)
    got_yl, mine, other = after(swap(got, "yl"), mine, other)
    got_last, got_core, other = swap(got_yl, "core"), swap(got, "core"), swap(other, "core")
    refreshed, upstream = pl.pallas_call(
        finish_kernel,
        out_shape=(
            jax.ShapeDtypeStruct((tokens, features), bf16),
            jax.ShapeDtypeStruct((tokens, width), bf16),
        ),
        in_specs=[SCALARS] + whole(7),
        out_specs=(whole(1)[0], pl.BlockSpec(memory_space=pl.ANY)),
        scratch_shapes=[
            pltpu.VMEM((rank, width), bf16),
            pltpu.VMEM((4 * z * EXTRA, LANES), bf16),
            pltpu.VMEM((tokens, width), bf16),
            pltpu.SemaphoreType.DMA,
        ],
        compiler_params=params,
        name="finish",
    )(place, got, got_yl, got_core, got_last, acts, mine, other)
    return (
        upstream[None],
        refreshed[None],
        down_new.T[None],
        down_first_new.T[None],
        down_second_new.T[None],
        up_new[None],
        up_first_new[None],
        up_second_new[None],
    )


def solution(mesh):
    sections, dp = mesh.devices.shape
    staged = Mesh(mesh.devices.reshape(sections, dp // 4, 2, 2), ("section", "z", "yl", "core"))
    split = P("section", ("z", "yl", "core"))
    return jax.shard_map(
        per_device,
        mesh=staged,
        in_specs=(split,) * 10 + (P(),),
        out_specs=(split,) * 8,
        check_vma=False,
    )
```

```python
import jax
import jax.numpy as jnp
from jax import lax
from jax.experimental import pallas as pl
from jax.experimental.pallas import tpu as pltpu
from jax.sharding import Mesh, PartitionSpec as P

adapter_scale = 2.0
beta_one = 0.9
beta_two = 0.999
learn_rate = 0.05
adam_eps = 1e-08

LANES = 128
EXTRA = 8
bf16 = jnp.bfloat16
f32 = jnp.float32
VMEM_BYTES = 20 * 1024 * 1024


def adam_update(master, first, second, grad, count):
    first_new = beta_one * first + (1.0 - beta_one) * grad
    second_new = beta_two * second + (1.0 - beta_two) * grad * grad
    fix_first = 1.0 - jnp.power(jnp.float32(beta_one), count)
    fix_second = 1.0 - jnp.power(jnp.float32(beta_two), count)
    master_new = master - learn_rate * (first_new / fix_first) / (
        jnp.sqrt(second_new / fix_second) + adam_eps
    )
    return (master_new, first_new, second_new)


def swap(array, axis):
    return lax.ppermute(array, axis, [(0, 1), (1, 0)])


def after(value, *others):
    return lax.optimization_barrier((value,) + others)


def spread(copies):
    return lax.all_to_all(copies, "z", 0, 0)


def pad_rows(parts, rows):
    have = sum(p.shape[0] for p in parts)
    if have < rows:
        parts = parts + [jnp.zeros((rows - have, LANES), parts[0].dtype)]
    return jnp.concatenate(parts, axis=0)


def nn(a, b):
    return jnp.dot(a, b, preferred_element_type=f32)


def nt(a, b):
    return lax.dot_general(a, b, (((1,), (1,)), ((), ())), preferred_element_type=f32)


def target_of(q, core, yl, z, rank, up_rows):
    j = q % EXTRA
    block = q // EXTRA
    of_core = jnp.where(block // (2 * z) == 0, core, 1 - core)
    of_yl = jnp.where((block // z) % 2 == 0, yl, 1 - yl)
    row = (block % z) * 4 + of_yl * 2 + of_core
    return jnp.where(j < up_rows, j * rank + row, jnp.where(j < up_rows + 2, up_rows * rank + j - up_rows, -1))


def unpack(core, yl, quarters, down, extra, rank):
    z = quarters[0].shape[0]
    for quarter, ref in enumerate(quarters):
        of_core = core if quarter < 2 else 1 - core
        of_yl = yl if quarter % 2 == 0 else 1 - yl
        offset = (of_yl * 2 + of_core) * LANES
        for i in range(z):
            at = pl.multiple_of(i * 4 * LANES + offset, LANES)
            down[:, pl.ds(at, LANES)] = ref[i, :rank, :]
            row = (quarter * z + i) * EXTRA
            extra[row : row + EXTRA, :] = ref[i, rank:, :]


def up_rows_of(core, yl, extra, z, rank, up_rows):
    places = up_rows * rank + 16
    shape = (places, extra.shape[0])
    q = lax.broadcasted_iota(jnp.int32, (1, shape[1]), 1)
    pick = lax.broadcasted_iota(jnp.int32, shape, 0) == target_of(q, core, yl, z, rank, up_rows)
    found = nn(pick.astype(f32).astype(bf16), extra[...])
    up = jnp.concatenate(
        [found[k * rank : (k + 1) * rank].astype(bf16) for k in range(up_rows)], axis=1
    )
    return up, found[up_rows * rank :]


def prepare_kernel(down_master, up_master, loss_weight, value_weight, copies, weights):
    rank = down_master.shape[0]
    features = up_master.shape[1]
    down = down_master[...].astype(bf16)
    count = jnp.sum(loss_weight[...].astype(f32), axis=1, keepdims=True)
    high = jnp.floor(count / 128.0)
    parts = [up_master[:, at : at + LANES] for at in range(0, features, LANES)]
    parts += [jnp.broadcast_to(c, (1, LANES)) for c in (high, count - 128.0 * high)]
    parts.append(jnp.zeros((EXTRA - len(parts), LANES), f32))
    extra = jnp.concatenate(parts, axis=0).astype(bf16)
    for i in range(copies.shape[0]):
        copies[i, :rank, :] = down
        copies[i, rank:, :] = extra
    weights[:features, :] = value_weight[...].astype(f32).T.astype(bf16)
    weights[features:, :] = down


def backward_kernel(
    place, q0, q1, q2, q3, acts, value_grad, loss_weight, keep, send, rows_out, down, extra
):
    core, yl = place[0], place[1]
    z = q0.shape[0]
    rank = down.shape[0]
    tokens, features = value_grad.shape
    up_rows = features // LANES
    unpack(core, yl, (q0, q1, q2, q3), down, extra, rank)
    up, counts = up_rows_of(core, yl, extra, z, rank, up_rows)
    total = counts[0:1, :1] * 128.0 + counts[1:2, :1]
    weight = jnp.broadcast_to(loss_weight[...].astype(f32), (tokens, tokens))
    square = (tokens, tokens)
    diagonal = lax.broadcasted_iota(jnp.int32, square, 0) == lax.broadcasted_iota(jnp.int32, square, 1)
    share = jnp.sum(jnp.where(diagonal, weight, 0.0), axis=1, keepdims=True) / total
    scaled = (value_grad[...].astype(f32) * share).astype(bf16)
    rows_out[:tokens, :features] = scaled
    rows_out[:tokens, features:] = (adapter_scale * nt(scaled, up)).astype(bf16)
    if rows_out.shape[0] > tokens:
        rows_out[tokens:, :] = jnp.zeros((rows_out.shape[0] - tokens, rows_out.shape[1]), bf16)
    mid_t = (adapter_scale * nt(up, scaled)).astype(bf16)
    low_t = nt(down[...], acts[...]).astype(bf16)

    shape = (extra.shape[0], up_rows * rank)
    q = lax.broadcasted_iota(jnp.int32, (shape[0], 1), 0)
    put = lax.broadcasted_iota(jnp.int32, shape, 1) == target_of(q, core, yl, z, rank, up_rows)
    put = put.astype(f32).astype(bf16)
    up_grad = jnp.zeros((shape[0], LANES), f32)
    for k in range(up_rows):
        low_k = nn(put[:, k * rank : (k + 1) * rank], low_t).astype(bf16)
        up_grad = up_grad + nn(low_k, scaled[:, k * LANES : (k + 1) * LANES])
    up_grad = adapter_scale * up_grad

    for half in range(2):
        of_yl = yl if half == 0 else 1 - yl
        for i in range(z):
            at = pl.multiple_of(i * 4 * LANES + of_yl * 2 * LANES, 2 * LANES)
            grad = nn(mid_t, acts[:, pl.ds(at, 2 * LANES)])
            first, second = grad[:, :LANES], grad[:, LANES:]
            row = (half * z + i) * EXTRA
            keep[half, i, :rank, :] = jnp.where(core == 0, first, second)
            keep[half, i, rank:, :] = up_grad[row : row + EXTRA]
            row = ((2 + half) * z + i) * EXTRA
            send[half, i, :rank, :] = jnp.where(core == 0, second, first).astype(bf16)
            send[half, i, rank:, :] = up_grad[row : row + EXTRA].astype(bf16)


def columns_kernel(rows_mine, rows_other, weights, mine, other, rows, held, sems):
    tokens, second = mine.shape[0], rows_mine.shape[0]
    chunks = sems.shape[0] - 2
    size = held.shape[0] // chunks
    copies = [
        pltpu.make_async_copy(rows_mine, rows.at[pl.ds(0, second)], sems.at[chunks]),
        pltpu.make_async_copy(rows_other, rows.at[pl.ds(second, second)], sems.at[chunks + 1]),
    ]
    for k in range(chunks):
        part = pl.ds(k * size, size)
        copies.append(pltpu.make_async_copy(weights.at[part], held.at[part], sems.at[k]))
    for copy in copies:
        copy.start()
    copies[0].wait()
    copies[1].wait()
    for k in range(chunks):
        copies[k + 2].wait()
        for i in range(k * size, (k + 1) * size, 2):
            product = nn(rows[...], jnp.concatenate([held[i], held[i + 1]], axis=1))
            mine[:, i * LANES : (i + 2) * LANES] = product[:tokens].astype(bf16)
            other[:, i * LANES : (i + 2) * LANES] = product[second : second + tokens].astype(bf16)


def finish_kernel(place, q0, q1, q23, acts, mine, other, out, upstream, down, extra, merged, sem):
    core, yl = place[0], place[1]
    rank = down.shape[0]
    for i in range(mine.shape[1] // LANES):
        a, b = mine[:, i * LANES : (i + 1) * LANES], other[:, i * LANES : (i + 1) * LANES]
        at = i * 2 * LANES
        merged[:, at : at + LANES] = jnp.where(core == 0, a, b)
        merged[:, at + LANES : at + 2 * LANES] = jnp.where(core == 0, b, a)
    copy = pltpu.make_async_copy(merged, upstream, sem)
    copy.start()
    unpack(core, yl, (q0, q1, q23.at[0], q23.at[1]), down, extra, rank)
    up, _ = up_rows_of(core, yl, extra, q0.shape[0], rank, out.shape[1] // LANES)
    low = nt(acts[...], down[...]).astype(bf16)
    out[...] = (adapter_scale * nn(low, up)).astype(bf16)
    copy.wait()


def whole(n):
    return [pl.BlockSpec(memory_space=pltpu.VMEM)] * n


SCALARS = pl.BlockSpec(memory_space=pltpu.SMEM)


def per_device(
    acts,
    value_grad,
    loss_weight,
    value_weight,
    down_master,
    down_first,
    down_second,
    up_master,
    up_first,
    up_second,
    step_count,
):
    tokens, width = acts.shape[1:]
    features = value_grad.shape[2]
    rank = down_master.shape[2]
    up_rows = features // LANES
    rows = rank + EXTRA
    padded = -(-tokens // 16) * 16
    z, sections = lax.axis_size("z"), lax.axis_size("section")
    place = jnp.stack([lax.axis_index("core"), lax.axis_index("yl")]).astype(jnp.int32)
    params = pltpu.CompilerParams(vmem_limit_bytes=VMEM_BYTES)
    acts = acts[0]
    copies, weights = pl.pallas_call(
        prepare_kernel,
        out_shape=(
            jax.ShapeDtypeStruct((z, rows, LANES), bf16),
            jax.ShapeDtypeStruct((features + rank, LANES), bf16),
        ),
        in_specs=whole(4),
        out_specs=tuple(whole(2)),
        compiler_params=pltpu.CompilerParams(vmem_limit_bytes=60 * 1024 * 1024),
        name="prepare",
    )(down_master[0].T, up_master[0], loss_weight, value_weight[0])

    def from_next(flip):
        return [
            (s * 2 + (yl ^ flip), (s - 1) * 2 + yl) for s in range(1, sections) for yl in range(2)
        ]

    same = lax.ppermute(weights, ("section", "yl"), from_next(0))
    flipped = lax.ppermute(weights, ("section", "yl"), from_next(1))

    got = spread(copies)
    even = lax.axis_index("yl") == 0
    weights = jnp.stack([jnp.where(even, same, flipped), jnp.where(even, flipped, same)])
    got, weights = after(got, weights)
    got_yl = swap(got, "yl")
    weights_all = lax.all_gather(weights, "z").reshape(2 * z, features + rank, LANES)

    keep, send, next_rows = pl.pallas_call(
        backward_kernel,
        out_shape=(
            jax.ShapeDtypeStruct((2, z, rows, LANES), f32),
            jax.ShapeDtypeStruct((2, z, rows, LANES), bf16),
            jax.ShapeDtypeStruct((padded, features + rank), bf16),
        ),
        in_specs=[SCALARS] + whole(7),
        out_specs=tuple(whole(3)),
        scratch_shapes=[
            pltpu.VMEM((rank, width), bf16),
            pltpu.VMEM((4 * z * EXTRA, LANES), bf16),
        ],
        compiler_params=params,
        name="backward",
    )(place, got, got_yl, swap(got, "core"), swap(got_yl, "core"), acts, value_grad[0], loss_weight)
    rows_mine, rows_other = [
        lax.ppermute(
            next_rows,
            ("section", "core"),
            [(s * 2 + (c ^ flip), (s - 1) * 2 + c) for s in range(1, sections) for c in range(2)],
        )
        for flip in range(2)
    ]

    kept = keep + swap(send, "core").astype(f32)
    kept = kept[0] + swap(kept[1].astype(bf16), "yl").astype(f32)
    parts = lax.all_to_all(kept.astype(bf16), "z", 0, 0)
    parts, rows_mine, rows_other = after(parts, rows_mine, rows_other)
    grad = jnp.sum(parts.astype(f32), axis=0)

    count = step_count.astype(f32)[0]
    down_new, down_first_new, down_second_new = adam_update(
        down_master[0].T, down_first[0].T, down_second[0].T, grad[:rank], count
    )
    up_new, up_first_new, up_second_new = adam_update(
        up_master[0], up_first[0], up_second[0], grad[rank : rank + up_rows].reshape(1, features), count
    )
    block = pad_rows([down_new.astype(bf16), up_new.astype(bf16).reshape(up_rows, LANES)], rows)
    got = spread(jnp.broadcast_to(block[None], (z, rows, LANES)))
    weights_all, _ = after(weights_all, got)
    chunks = min(4, z)
    half = jax.ShapeDtypeStruct((tokens, width // 2), bf16)
    mine, other = pl.pallas_call(
        columns_kernel,
        out_shape=(half, half),
        in_specs=[pl.BlockSpec(memory_space=pl.ANY)] * 3,
        out_specs=tuple(whole(2)),
        scratch_shapes=[
            pltpu.VMEM((2 * padded, features + rank), bf16),
            pltpu.VMEM((2 * z, features + rank, LANES), bf16),
            pltpu.SemaphoreType.DMA((chunks + 2,)),
        ],
        compiler_params=pltpu.CompilerParams(vmem_limit_bytes=52 * 1024 * 1024),
        cost_estimate=pl.CostEstimate(
            flops=2 * tokens * (features + rank) * width,
            bytes_accessed=(features + rank) * width,
            transcendentals=0,
        ),
        name="columns",
    )(rows_mine, rows_other, weights_all)
    got_yl, mine, other = after(swap(got, "yl"), mine, other)
    got_core, other = swap(jnp.stack([got, got_yl]), "core"), swap(other, "core")
    refreshed, upstream = pl.pallas_call(
        finish_kernel,
        out_shape=(
            jax.ShapeDtypeStruct((tokens, features), bf16),
            jax.ShapeDtypeStruct((tokens, width), bf16),
        ),
        in_specs=[SCALARS] + whole(6),
        out_specs=(whole(1)[0], pl.BlockSpec(memory_space=pl.ANY)),
        scratch_shapes=[
            pltpu.VMEM((rank, width), bf16),
            pltpu.VMEM((4 * z * EXTRA, LANES), bf16),
            pltpu.VMEM((tokens, width), bf16),
            pltpu.SemaphoreType.DMA,
        ],
        compiler_params=params,
        name="finish",
    )(place, got, got_yl, got_core, acts, mine, other)
    return (
        upstream[None],
        refreshed[None],
        down_new.T[None],
        down_first_new.T[None],
        down_second_new.T[None],
        up_new[None],
        up_first_new[None],
        up_second_new[None],
    )


def solution(mesh):
    sections, dp = mesh.devices.shape
    staged = Mesh(mesh.devices.reshape(sections, dp // 4, 2, 2), ("section", "z", "yl", "core"))
    split = P("section", ("z", "yl", "core"))
    return jax.shard_map(
        per_device,
        mesh=staged,
        in_specs=(split,) * 10 + (P(),),
        out_specs=(split,) * 8,
        check_vma=False,
    )
```
